256 devices in a mesh: pre: 16 (over z, core), grp: 4 (over y), kv: 4 (over x).
Axes of the slice: x: 4, y: 4, z: 8, core: 2. Of those that a mesh axis runs over, the one named last changes fastest.
Arguments:
- prefill_kv: bfloat16 [1024, 2, 8, 64, 128], P(('pre', 'grp'), None, 'kv'), may hold values from -6 to 6
- page_match: int32 [64, 64, 1], P(('pre', 'grp')), may hold values from 0 to 15
- queries: bfloat16 [512, 4, 128, 128], P(('pre', 'grp'), None, 'kv'), may hold values from -192 to 192
- new_kv: bfloat16 [512, 4, 2, 8, 128], P(('pre', 'grp'), None, None, 'kv'), may hold values from -6 to 6
- slot_request: int32 [128, 4], P('pre', 'grp'), may hold values from 0 to 511, as said below
- page_table: int32 [128, 4, 32], P('pre', 'grp'), may hold values from 0 to 63
- context_len: int32 [128, 4], P('pre', 'grp'), may hold values from 1 to 2048, as said below
- out_weight: bfloat16 [16384, 16384], P('kv', 'pre'), may hold values from -0.1875 to 0.1875
Outputs:
- decoded: bfloat16 [128, 4, 4, 16384], P(None, 'grp', None, ('pre', 'kv'))
The draws below stay inside these ranges and needn't reach their ends.
Inputs may be any that keep to these rules, and one draw needn't show every extreme that they name: `slot_request`: every request is served by exactly one slot. Requests r with the same r // 2 are served by one decode device, and every decode device serves exactly 2 requests of a source device s (requests s * 8 .. (s + 1) * 8 - 1) or none. `context_len`: some slot's context is exactly 2048 positions long.
All inputs are finite; a program needn't handle non-finite values.
Results may differ from the reference program's by a relative error of at most 0.0052.
Values may be sent and summed in bfloat16 or wider, within the bound.
A program may use at most 128 MiB of HBM per device.

```python
import jax
import jax.numpy as jnp
from jax import lax

D = 16384
QH = 128
KVH = 8
HD = 128
PAGE = 64
STEPS = 4
MAXP = 32
POOL_DEV = 64
QCAP = 2
PAGES_DEV = 16
REQ_DEV = 8
SHARDS = 64
CAP = 1
PAGES = 1024
GROUPS = 4
GSLOTS = 128
REQS = 512
N_PRE = 16
N_GRP = 4


def draw_queries(key, part):
    key = jax.random.fold_in(key, 5)
    values = jnp.clip(2.0 * jax.random.normal(key, (REQS, STEPS, QH, HD), jnp.float32), -12.0, 12.0)
    return values.astype(jnp.bfloat16)


def draw_new_kv(key, part):
    key = jax.random.fold_in(key, 6)
    drawn = jnp.clip(jax.random.normal(key, (REQS, STEPS, 2, KVH, HD), jnp.float32), -6.0, 6.0)
    return drawn.astype(jnp.bfloat16)


def draw_slot_request(key, part):
    key = jax.random.fold_in(key, 7)
    first_order = jax.random.permutation(jax.random.fold_in(key, 1), SHARDS).astype(jnp.int32)
    second_order = jax.random.permutation(jax.random.fold_in(key, 2), SHARDS).astype(jnp.int32)
    blocks = REQ_DEV // QCAP
    flips = jax.random.randint(jax.random.fold_in(key, 3), (SHARDS, blocks), 0, QCAP, dtype=jnp.int32)
    device_ids = jnp.arange(SHARDS, dtype=jnp.int32)[:, None]
    slot_ids = jnp.arange(REQ_DEV, dtype=jnp.int32)[None, :]
    block_ids = slot_ids // QCAP
    within = (slot_ids % QCAP + jnp.repeat(flips, QCAP, axis=1)) % QCAP
    sources = first_order[(second_order[device_ids] - block_ids) % SHARDS]
    requests = sources * REQ_DEV + block_ids * QCAP + within
    pre_count = GSLOTS // REQ_DEV
    requests = requests.reshape(pre_count, GROUPS, REQ_DEV).transpose(0, 2, 1).reshape(GSLOTS, GROUPS)
    return requests.astype(jnp.int32)


def draw_context_len(key, part):
    key = jax.random.fold_in(key, 8)
    lengths = jax.random.randint(key, (GSLOTS * GROUPS,), 1, MAXP * PAGE + 1, dtype=jnp.int32)
    longest_at = jax.random.randint(jax.random.fold_in(key, 1), (), 0, GSLOTS * GROUPS, dtype=jnp.int32)
    flattened = jnp.where(jnp.arange(GSLOTS * GROUPS, dtype=jnp.int32) == longest_at, MAXP * PAGE, lengths)
    return flattened.astype(jnp.int32).reshape(GSLOTS, GROUPS)


def touch_ends(values, own_key, smallest, high):
    shape = values.shape
    place = [jax.random.randint(jax.random.fold_in(own_key, axis), (), 0, shape[axis]) for axis in range(len(shape))]
    values = values.at[tuple(place)].set(smallest)
    longest = shape.index(max(shape))
    place[longest] = (place[longest] + 1) % shape[longest]
    return values.at[tuple(place)].set(high)


def steps_of(stream_key, shape, split, smallest, top_value):
    def one(position, parts):
        heights = jax.random.uniform(jax.random.fold_in(jax.random.fold_in(stream_key, 6), position), (parts,), jnp.float32, smallest / len(split), top_value / len(split))
        return jnp.repeat(jnp.exp(heights), shape[position] // parts).reshape((-1,) + (1,) * (len(shape) - position - 1))

    factor_of = one(*split[0])
    for cut in split[1:]:
        factor_of = factor_of * one(*cut)
    return factor_of


def scatter_about(own_key, dims, width, reach, cuts=(), kind=jnp.bfloat16):
    drawn = width * jax.random.normal(own_key, dims, jnp.float32)
    if cuts:
        drawn = drawn * steps_of(own_key, dims, cuts, -0.22, 0.18)
    return jnp.clip(drawn, -reach, reach).astype(kind)


def setup_inputs(seed: int = 0) -> dict:
    arg_keys = jax.random.split(jax.random.key(seed), 9)
    prefill_kv = scatter_about(arg_keys[0], (PAGES, 2, KVH, PAGE, HD), 1.0, 6.0, ((0, 64), (2, 4)))
    page_match = touch_ends(jax.random.randint(arg_keys[1], (SHARDS, SHARDS, CAP), 0, PAGES_DEV), jax.random.fold_in(arg_keys[1], 1), 0, PAGES_DEV - 1).astype(jnp.int32)
    queries = draw_queries(jax.random.fold_in(arg_keys[8], 71), 0)
    new_kv = draw_new_kv(jax.random.fold_in(arg_keys[8], 71), 0)
    slot_request = draw_slot_request(jax.random.fold_in(arg_keys[8], 71), 0)
    page_table = touch_ends(jax.random.randint(arg_keys[5], (GSLOTS, GROUPS, MAXP), 0, POOL_DEV), jax.random.fold_in(arg_keys[5], 1), 0, POOL_DEV - 1).astype(jnp.int32)
    context_len = draw_context_len(jax.random.fold_in(arg_keys[8], 71), 0)
    out_weight = scatter_about(arg_keys[7], (QH * HD, D), (QH * HD // 16) ** -0.5, 0.1875, ((0, 4), (1, 16)))
    return dict(prefill_kv=prefill_kv, page_match=page_match, queries=queries, new_kv=new_kv, slot_request=slot_request, page_table=page_table, context_len=context_len, out_weight=out_weight)


NEG_FILL = -1.0e30


def reference(prefill_kv, page_match, queries, new_kv, slot_request, page_table, context_len, out_weight):
    shards = N_PRE * N_GRP
    per_cap = POOL_DEV // shards
    heads_per = QH // KVH
    scale_qk = 1.0 / (HD ** 0.5)
    rows_q = STEPS * heads_per
    span_all = MAXP * PAGE
    positions = jnp.arange(span_all, dtype=jnp.int32)
    step_rows = jnp.arange(rows_q, dtype=jnp.int32) // heads_per
    new_valid = jnp.arange(STEPS, dtype=jnp.int32)[None, :] <= step_rows[:, None]

    def one_slot(indices):
        slot_id = indices[0]
        group_id = indices[1]
        device = (slot_id // REQ_DEV) * N_GRP + group_id
        page_ids = page_table[slot_id, group_id]
        source = page_ids // per_cap
        offset = page_ids % per_cap
        local_page = page_match[source, device, offset]
        fetched = prefill_kv[(source * PAGES_DEV + local_page).astype(jnp.int32)]
        request = slot_request[slot_id, group_id]
        query_f = queries[request].astype(jnp.float32)
        query_f = query_f.reshape(STEPS, KVH, heads_per, HD).transpose(1, 0, 2, 3).reshape(KVH, rows_q, HD)
        fresh_kv = new_kv[request].astype(jnp.float32)
        cache_keys = fetched[:, 0].astype(jnp.float32)
        cache_vals = fetched[:, 1].astype(jnp.float32)
        cache_scores = jnp.einsum("hqd,phkd->hqpk", query_f, cache_keys).reshape(KVH, rows_q, span_all) * scale_qk
        new_scores = jnp.einsum("hqd,uhd->hqu", query_f, fresh_kv[:, 0]) * scale_qk
        length = context_len[slot_id, group_id]
        cache_valid = positions < length
        cache_scores = jnp.where(cache_valid[None, None, :], cache_scores, NEG_FILL)
        new_scores = jnp.where(new_valid[None], new_scores, NEG_FILL)
        highest = jnp.maximum(jnp.max(cache_scores, axis=-1), jnp.max(new_scores, axis=-1))
        cache_w = jnp.where(cache_valid[None, None, :], jnp.exp(cache_scores - highest[..., None]), 0.0)
        new_w = jnp.where(new_valid[None], jnp.exp(new_scores - highest[..., None]), 0.0)
        totals = jnp.sum(cache_w, axis=-1) + jnp.sum(new_w, axis=-1)
        cache_wb = lax.optimization_barrier(cache_w.astype(jnp.bfloat16)).astype(jnp.float32)
        cache_wb = cache_wb.reshape(KVH, rows_q, MAXP, PAGE)
        new_wb = lax.optimization_barrier(new_w.astype(jnp.bfloat16)).astype(jnp.float32)
        weighted = jnp.einsum("hqpk,phkd->hqd", cache_wb, cache_vals) + jnp.einsum("hqu,uhd->hqd", new_wb, fresh_kv[:, 1])
        attended = (weighted / totals[..., None]).astype(jnp.bfloat16)
        return attended.reshape(KVH, STEPS, heads_per, HD).transpose(1, 0, 2, 3).reshape(STEPS, QH * HD)

    slot_grid, group_grid = jnp.meshgrid(jnp.arange(GSLOTS, dtype=jnp.int32), jnp.arange(GROUPS, dtype=jnp.int32), indexing="ij")
    slot_pairs = jnp.stack([slot_grid.reshape(-1), group_grid.reshape(-1)], axis=1).astype(jnp.int32)
    attention = lax.map(one_slot, slot_pairs)
    flattened = attention.reshape(GSLOTS * GROUPS * STEPS, QH * HD)
    output = jnp.dot(flattened, out_weight, preferred_element_type=jnp.float32).astype(jnp.bfloat16)
    return output.reshape(GSLOTS, GROUPS, STEPS, D)
```

```python
import functools

import jax
import jax.numpy as jnp
from jax import lax
from jax.experimental import pallas as pl
from jax.experimental.pallas import tpu as pltpu
from jax.sharding import PartitionSpec as P

MESH = pl.DeviceIdType.MESH
HD = 128
PAGE = 64
STEPS = 4
MAXP = 32
NZ = 8
NM = 8
LOG2E = 1.4426950408889634
SCALE = LOG2E / HD**0.5
DEAD = -1e30
MIB = 1 << 20
NG = 4
NT = (((1,), (1,)), ((), ()))


def here():
    p = lax.axis_index("pre")
    return p // 2, p % 2, lax.axis_index("grp")


def dev(z, c, y):
    return {"pre": z * 2 + c, "grp": y}


def dev_zm(z, m):
    return dev(z, m // 4, m % 4)


def wrap(a, n):
    return lax.rem(a + 2 * n, n)


def remote(src, dst, ssem, rsem, device):
    return pltpu.make_async_remote_copy(
        src_ref=src, dst_ref=dst, send_sem=ssem, recv_sem=rsem, device_id=device, device_id_type=MESH
    )


def split3(x):
    hi = x.astype(jnp.bfloat16).astype(jnp.float32)
    mid = (x - hi).astype(jnp.bfloat16).astype(jnp.float32)
    return hi, mid, x - hi - mid


def merge(a, b):
    acc_a, m_a, l_a = a
    acc_b, m_b, l_b = b
    top = jnp.maximum(m_a, m_b)
    fa = jnp.exp2(m_a - top)
    fb = jnp.exp2(m_b - top)
    return acc_a * fa + acc_b * fb, top, l_a * fa + l_b * fb


def attend_kernel(
    qx, ti, mm, pg, out,
    i1, sb, sbn, qg, ng, tig, mmv, mms, pgs, kd, vt, bi, rs_out, rs_in,
    p1s, p1r, tis, tir, mss, msr, loc, ys, yr, ys2, yr2, cs, cr, p2s, p2r, p3s, p3r, as_, ar, rss, rsr,
):
    z, c, y = here()
    me_m = c * 4 + y

    bar = pltpu.get_barrier_semaphore()

    def greet(k, carry):
        j = lax.rem(z * 8 + me_m + k, 64)
        pl.semaphore_signal(bar, inc=1, device_id=dev_zm(j // 8, j % 8), device_id_type=MESH)
        return carry

    lax.fori_loop(1, 64, greet, 0)

    own_pages = pltpu.make_async_copy(pg, pgs.at[me_m], loc.at[0])
    own_pages.start()
    i1[z, me_m] = qx[z, me_m]
    tig[z] = ti[...]
    mmv[me_m] = mm[...]
    pl.semaphore_wait(bar, 63)

    def spread(kz, km):
        zj = lax.rem(z + kz, 8)
        mj = lax.rem(me_m + km, 8)
        k = kz * 8 + km
        return remote(qx.at[zj, mj], i1.at[z, me_m], p1s.at[k], p1r.at[k], dev_zm(zj, mj))

    def start_spread(kz, lo):
        def one(km, carry):
            spread(kz, km).start()
            return carry

        lax.fori_loop(lo, 8, one, 0)

    for kz in (4, 3, 5, 2, 6, 1, 7):
        start_spread(kz, 0)
    start_spread(0, 1)

    def table_copy(kz):
        zj = lax.rem(z + kz, 8)
        return remote(ti, tig.at[z], tis.at[kz], tir.at[kz], dev(zj, c, y))

    def match_copy(km):
        mj = lax.rem(me_m + km, 8)
        return remote(mm, mmv.at[me_m], mss.at[km], msr.at[km], dev_zm(z, mj))

    def start_small(k, carry):
        table_copy(k).start()
        match_copy(k).start()
        return carry

    lax.fori_loop(1, 8, start_small, 0)

    y_up, y_dn = wrap(y + 1, 4), wrap(y - 1, 4)

    def m_of(cc, yy):
        return cc * 4 + wrap(yy, 4)

    def quarter(m, q):
        return pgs.at[m, pl.ds(4 * q, 4)]

    def y_copy(direction, q):
        target = dev(z, c, y_up if direction == 0 else y_dn)
        return remote(pg.at[pl.ds(4 * q, 4)], quarter(me_m, q), ys.at[direction, q], yr.at[direction, q], target)

    def y_far(direction, q):
        target = dev(z, c, y_up if direction == 0 else y_dn)
        m = m_of(c, y - 1 if direction == 0 else y + 1)
        return remote(quarter(m, q), quarter(m, q), ys2.at[q], yr2.at[q], target)

    def core_copy(dy, q):
        m = m_of(c, y + dy)
        src = pg.at[pl.ds(4 * q, 4)] if dy == 0 else quarter(m, q)
        return remote(src, quarter(m, q), cs.at[dy, q], cr.at[dy, q], dev(z, 1 - c, y))

    order = ((0, 1, 2, 3), (2, 3, 0, 1))
    for n in range(4):
        for direction in range(2):
            y_copy(direction, order[direction][n]).start()
    for q in range(4):
        core_copy(0, q).start()

    def wait_spread_kz(kz, lo):
        def one(km, carry):
            spread(kz, km).wait_recv()
            return carry

        lax.fori_loop(lo, 8, one, 0)

    wait_spread_kz(0, 1)
    for kz in (1, 7, 2, 6, 3, 5, 4):
        wait_spread_kz(kz, 0)

    arrived = i1[...].astype(jnp.float32).reshape(64, 32, 128)
    table = jnp.concatenate(
        [arrived[:, 0:8].reshape(512, 128), arrived[:, 8:16].reshape(512, 128), arrived[:, 16:24].reshape(512, 128)],
        axis=1,
    ).astype(jnp.bfloat16)
    ids = arrived[:, 24:32].reshape(512, 128)
    request = (ids[:, 0:1] * 8.0 + ids[:, 64:65]).astype(jnp.int32)
    hot = (request == lax.broadcasted_iota(jnp.int32, (512, 512), 1)).astype(jnp.float32).astype(jnp.bfloat16)
    moved = jnp.dot(hot, table, preferred_element_type=jnp.float32).reshape(8, 8, 8, 384)
    for m in range(8):
        for d in range(8):
            rows = moved[d, m]
            sb[m, d] = jnp.concatenate([rows[:, 0:128], rows[:, 128:256]], axis=0).astype(jnp.bfloat16)
        for d in range(0, 8, 2):
            pair = jnp.concatenate([moved[d, m][:, 256:384], moved[d + 1, m][:, 256:384]], axis=0)
            sbn[m, d // 2] = pair.astype(jnp.bfloat16)

    def to_slots(km):
        mj = lax.rem(me_m + km, 8)
        return (
            remote(sb.at[mj], qg.at[z, me_m], p2s.at[km], p2r.at[km], dev_zm(z, mj)),
            remote(sbn.at[mj], ng.at[me_m], p3s.at[km], p3r.at[km], dev_zm(z, mj)),
        )

    def start_slots(km, carry):
        for copy in to_slots(km):
            copy.start()
        return carry

    lax.fori_loop(1, 8, start_slots, 0)
    qg[z, me_m] = sb[me_m]
    ng[me_m] = sbn[me_m]

    for n in range(2):
        for direction in range(2):
            q = order[direction][n]
            y_copy(direction, q).wait_recv()
            y_far(direction, q).start()
            core_copy(3 if direction == 0 else 1, q).start()

    def wait_slots(km, carry):
        for copy in to_slots(km):
            copy.wait_recv()
        return carry

    lax.fori_loop(1, 8, wait_slots, 0)

    z_up, z_dn = wrap(z + 1, 8), wrap(z - 1, 8)

    def around(direction, step):
        sign = 1 if direction == 0 else -1
        o = wrap(z - sign * (step - 1), 8)
        target = dev(z_up if direction == 0 else z_dn, c, y)
        if step < 4:
            part = qg.at[o]
        else:
            part = qg.at[o, :, pl.ds(4 * direction, 4)]
        return remote(part, part, as_.at[direction, step - 1], ar.at[direction, step - 1], target)

    for direction in range(2):
        around(direction, 1).start()

    for n in range(2, 4):
        for direction in range(2):
            q = order[direction][n]
            y_copy(direction, q).wait_recv()
            core_copy(3 if direction == 0 else 1, q).start()

    def wait_small(k, carry):
        table_copy(k).wait_recv()
        match_copy(k).wait_recv()
        return carry

    lax.fori_loop(1, 8, wait_small, 0)
    to_smem = pltpu.make_async_copy(mmv, mms, loc.at[1])
    to_smem.start()

    def biases(d, carry):
        rows = tig[d].astype(jnp.float32)
        pages = rows[0:32]
        whole = rows[32:33]
        rest = rows[33:34]
        slot = lax.broadcasted_iota(jnp.int32, (32, 128), 0).astype(jnp.float32)
        before = (slot < whole).astype(jnp.float32)
        at = (slot == whole).astype(jnp.float32)
        within = lax.broadcasted_iota(jnp.int32, (PAGE, 128), 0).astype(jnp.float32) < rest
        for m in range(8):
            same = (pages == (z * 8 + m).astype(jnp.float32)).astype(jnp.float32)
            full = jnp.sum(same * before, axis=0, keepdims=True)
            more = full + jnp.sum(same * at, axis=0, keepdims=True)
            low = jnp.where(full > 0.0, jnp.log(jnp.maximum(full, 1.0)) * LOG2E, DEAD)
            high = jnp.where(more > 0.0, jnp.log(jnp.maximum(more, 1.0)) * LOG2E, DEAD)
            bi[d, m * PAGE : (m + 1) * PAGE, :] = jnp.where(within, high, low)
        return carry

    lax.fori_loop(0, 8, biases, 0)

    for step in (1, 2):
        for direction in range(2):
            around(direction, step).wait_recv()
            around(direction, step + 1).start()

    for q in range(4):
        y_far(0 if q < 2 else 1, q).wait_recv()
        core_copy(2, q).start()
    for dy in range(4):
        for q in range(4):
            core_copy(dy, q).wait_recv()
    own_pages.wait()
    to_smem.wait()

    eye = (
        lax.broadcasted_iota(jnp.int32, (128, 128), 0) == lax.broadcasted_iota(jnp.int32, (128, 128), 1)
    ).astype(jnp.float32).astype(jnp.bfloat16)

    def select_pages(d, carry):
        for pair in range(4):
            picks = [mms[2 * pair + k, 0, d * 8 + me_m] for k in range(2)]
            for h in range(2):
                values = []
                for k in range(2):
                    m = 2 * pair + k
                    kd[d, h, m * PAGE : (m + 1) * PAGE, :] = pgs[m, picks[k], 0, h]
                    values.append(pgs[m, picks[k], 1, h])
                turned = lax.dot_general(
                    eye, jnp.concatenate(values, axis=0), NT, preferred_element_type=jnp.float32
                )
                vt[d, h, :, pair * 128 : (pair + 1) * 128] = turned.astype(jnp.bfloat16)
        return carry

    lax.fori_loop(0, 8, select_pages, 0)

    def unit(o, d):
        h = o // 4
        q = qg[o, :, d].reshape(128, 128)
        s = lax.dot_general(kd[d, h], q, NT, preferred_element_type=jnp.float32)
        s = s * SCALE + bi[d]
        top = jnp.max(s, axis=0, keepdims=True)
        w = jnp.exp2(s - top)
        total = jnp.sum(w, axis=0, keepdims=True)
        acc = jnp.dot(vt[d, h], w.astype(jnp.bfloat16), preferred_element_type=jnp.float32)
        return acc, top, total

    row16 = lax.broadcasted_iota(jnp.int32, (16, 128), 0)

    def pack(direction, k, d, part):
        acc, top, total = part
        rs_out[direction, k, d, 0:128, :] = acc.astype(jnp.bfloat16)
        stats = jnp.zeros((16, 128), jnp.float32)
        for n, row in enumerate(split3(top) + split3(total)):
            stats = jnp.where(row16 == n, row, stats)
        rs_out[direction, k, d, 128:144, :] = stats.astype(jnp.bfloat16)

    def unpack(direction, k, d):
        acc = rs_in[direction, k, d, 0:128, :].astype(jnp.float32)
        st = rs_in[direction, k, d, 128:144, :].astype(jnp.float32)
        return acc, st[0:1] + st[1:2] + st[2:3], st[3:4] + st[4:5] + st[5:6]

    def back(direction, k, d):
        target = dev(z_dn if direction == 0 else z_up, c, y)
        return remote(
            rs_out.at[direction, k - 1, d], rs_in.at[direction, k - 1, d],
            rss.at[direction, k - 1, d], rsr.at[direction, k - 1, d], target,
        )

    for direction in range(2):
        around(direction, 3).wait_recv()
        around(direction, 4).start()
    for direction in range(2):
        around(direction, 4).wait_recv()

    far = lax.rem(z + 4, 8)

    for direction in range(2):
        def far_step(d, carry):
            pack(direction, 3, d, unit(far, d))
            back(direction, 4, d).start()
            return carry

        lax.fori_loop(4 * direction, 4 * direction + 4, far_step, 0)

    for k in (3, 2, 1):
        for direction in range(2):
            o = wrap(z - k if direction == 0 else z + k, 8)
            lo, hi = (4 * direction, 4 * direction + 4) if k == 3 else (0, 8)

            def with_in(d, carry):
                part = unit(o, d)
                back(direction, k + 1, d).wait_recv()
                pack(direction, k - 1, d, merge(part, unpack(direction, k, d)))
                back(direction, k, d).start()
                return carry

            def without(d, carry):
                pack(direction, k - 1, d, unit(o, d))
                back(direction, k, d).start()
                return carry

            lax.fori_loop(lo, hi, with_in, 0)
            if k == 3:
                lax.fori_loop(4 - lo, 8 - lo, without, 0)

    lane = lax.broadcasted_iota(jnp.int32, (64, 128), 1)
    nrow = lax.broadcasted_iota(jnp.int32, (64, 128), 0)

    def finish(d, carry):
        part = unit(z, d)
        q = qg[z, :, d].reshape(128, 128)
        keys = jnp.concatenate([ng[2 * u, d // 2] for u in range(4)], axis=0)
        vals = jnp.concatenate([ng[2 * u + 1, d // 2] for u in range(4)], axis=0)
        s = lax.dot_general(keys, q, NT, preferred_element_type=jnp.float32) * SCALE
        valid = (
            ((nrow // 8) % 2 == d % 2) & (nrow % 8 == lane % 8) & (nrow // 16 <= (lane // 8) % 4)
        )
        s = jnp.where(valid, s, DEAD)
        top = jnp.max(s, axis=0, keepdims=True)
        w = jnp.exp2(s - top)
        total = jnp.sum(w, axis=0, keepdims=True)
        turned = lax.dot_general(eye, vals, NT, preferred_element_type=jnp.float32).astype(jnp.bfloat16)
        acc = jnp.dot(turned, w.astype(jnp.bfloat16), preferred_element_type=jnp.float32)
        part = merge(part, (acc, top, total))
        for direction in range(2):
            back(direction, 1, d).wait_recv()
            part = merge(part, unpack(direction, 0, d))
        acc, _, total = part
        rows = jnp.transpose(acc / total).astype(jnp.bfloat16)
        for h in range(4):
            out[h, d] = rows[h * 32 : (h + 1) * 32]
        return carry

    lax.fori_loop(0, 8, finish, 0)

    def wait_spread_send(k, carry):
        spread(k // 8, k % 8).wait_send()
        return carry

    lax.fori_loop(1, 64, wait_spread_send, 0)

    def wait_small_send(k, carry):
        table_copy(k).wait_send()
        match_copy(k).wait_send()
        for copy in to_slots(k):
            copy.wait_send()
        return carry

    lax.fori_loop(1, 8, wait_small_send, 0)
    for q in range(4):
        for direction in range(2):
            y_copy(direction, q).wait_send()
        y_far(0 if q < 2 else 1, q).wait_send()
        for dy in range(4):
            core_copy(dy, q).wait_send()
    for direction in range(2):
        for step in range(1, 5):
            around(direction, step).wait_send()

        def wait_back(d, carry):
            for k in (1, 2, 3):
                back(direction, k, d).wait_send()
            return carry

        lax.fori_loop(0, 8, wait_back, 0)

        def wait_far(d, carry):
            back(direction, 4, d).wait_send()
            return carry

        lax.fori_loop(4 * direction, 4 * direction + 4, wait_far, 0)


def attend(qx, ti, mm, pages):
    bf, f32 = jnp.bfloat16, jnp.float32
    vm = pltpu.VMEM
    dma = pltpu.SemaphoreType.DMA
    return pl.pallas_call(
        attend_kernel,
        out_shape=jax.ShapeDtypeStruct((4, 8, 32, 128), bf),
        in_specs=[pl.BlockSpec(memory_space=pltpu.VMEM)] * 4,
        out_specs=pl.BlockSpec(memory_space=pltpu.VMEM),
        scratch_shapes=[
            vm((8, 8, 32, 128), bf),
            vm((8, 8, 16, 128), bf),
            vm((8, 4, 16, 128), bf),
            vm((8, 8, 8, 16, 128), bf),
            vm((8, 4, 16, 128), bf),
            vm((8, 48, 128), bf),
            vm((8, 1, 128), jnp.int32),
            pltpu.SMEM((8, 1, 128), jnp.int32),
            vm((8, 16, 2, 2, PAGE, 128), bf),
            vm((8, 2, 512, 128), bf),
            vm((8, 2, 128, 512), bf),
            vm((8, 512, 128), f32),
            vm((2, 4, 8, 144, 128), bf),
            vm((2, 4, 8, 144, 128), bf),
            dma((64,)), dma((64,)),
            dma((8,)), dma((8,)),
            dma((8,)), dma((8,)),
            dma((2,)),
            dma((2, 4)), dma((2, 4)),
            dma((4,)), dma((4,)),
            dma((4, 4)), dma((4, 4)),
            dma((8,)), dma((8,)),
            dma((8,)), dma((8,)),
            dma((2, 4)), dma((2, 4)),
            dma((2, 4, 8)), dma((2, 4, 8)),
        ],
        compiler_params=pltpu.CompilerParams(
            collective_id=1, has_side_effects=True, vmem_limit_bytes=48 * MIB
        ),
        name="attend",
    )(qx, ti, mm, pages)


def project_kernel(a, w_hbm, out, w, g, acc, xs, xr, wsem, zs, zr, cs, cr, xss, xsr):
    z, c, y = here()
    kx = lax.axis_index("kv")
    z_up, z_dn = wrap(z + 1, 8), wrap(z - 1, 8)
    w_copy = pltpu.make_async_copy(w_hbm, w, wsem.at[0])
    w_copy.start()
    bar = pltpu.get_barrier_semaphore()
    for target in (dev(z_up, c, y), dev(z_dn, c, y), dev(z, 1 - c, y)):
        pl.semaphore_signal(bar, inc=1, device_id=target, device_id_type=MESH)
    for dx in range(1, 4):
        pl.semaphore_signal(bar, inc=1, device_id={"kv": wrap(kx + dx, 4)}, device_id_type=MESH)
    ds = 8 // NG
    own = [pltpu.make_async_copy(a, g.at[c, z], wsem.at[1])]
    own[0].start()
    pl.semaphore_wait(bar, 6)

    def rows(ref, r):
        return ref.at[:, pl.ds(r * ds, ds)]

    def around(direction, step, r):
        sign = 1 if direction == 0 else -1
        o = wrap(z - sign * (step - 1), 8)
        target = dev(z_up if direction == 0 else z_dn, c, y)
        if step == 1:
            return remote(rows(a, r), rows(g.at[c, o], r), zs.at[direction, 0, r], zr.at[direction, 0, r], target)
        part = g.at[c, o]
        part = rows(part, r) if step < 4 else part.at[pl.ds(2 * direction, 2), pl.ds(r * ds, ds)]
        return remote(part, part, zs.at[direction, step - 1, r], zr.at[direction, step - 1, r], target)

    def across(dz, r):
        o = wrap(z + dz, 8)
        src = rows(a, r) if dz == 0 else rows(g.at[c, o], r)
        return remote(src, rows(g.at[c, o], r), cs.at[dz, r], cr.at[dz, r], dev(z, 1 - c, y))

    for r in range(NG):
        for direction in range(2):
            around(direction, 1, r).start()
        across(0, r).start()

    w_copy.wait()
    own[0].wait()

    def exchange(dx, r):
        return remote(
            xs.at[dx - 1, r], xr.at[dx - 1, r], xss.at[dx - 1, r], xsr.at[dx - 1, r], {"kv": wrap(kx + dx, 4)}
        )

    def use(o, r, first):
        o = wrap(o, 8)
        block = g[:, o, :, pl.ds(r * ds, ds)].reshape(2, 4, ds * 32, 128)
        left = jnp.concatenate(
            [jnp.concatenate([block[cc, h] for h in range(4)], axis=1) for cc in range(2)], axis=0
        )
        step = jnp.dot(
            left, w[pl.ds(pl.multiple_of(o * 512, 512), 512), :], preferred_element_type=jnp.float32
        )
        if first:
            acc[r] = step
        else:
            acc[r] += step

    def send_sums(r):
        for dx in range(1, 4):
            kk = wrap(kx + dx, 4)
            xs[dx - 1, r] = acc[r, :, pl.ds(pl.multiple_of(kk * 256, 256), 256)].astype(jnp.bfloat16)
            exchange(dx, r).start()

    def add_sums(r):
        total = acc[r, :, pl.ds(pl.multiple_of(kx * 256, 256), 256)]
        for dx in range(1, 4):
            exchange(dx, r).wait_recv()
            total = total + xr[dx - 1, r].astype(jnp.float32)
        out[:, pl.ds(r * ds, ds)] = total.astype(jnp.bfloat16).reshape(2, ds, 32, 256)

    for r in range(NG):
        across(0, r).wait_recv()
        use(z, r, True)
        for step in range(1, 4):
            for direction in range(2):
                sign = 1 if direction == 0 else -1
                around(direction, step, r).wait_recv()
                around(direction, step + 1, r).start()
                across((-sign * step) % 8, r).start()
            for direction in range(2):
                sign = 1 if direction == 0 else -1
                across((-sign * step) % 8, r).wait_recv()
                use(z - sign * step, r, False)
        for direction in range(2):
            around(direction, 4, r).wait_recv()
        across(4, r).start()
        across(4, r).wait_recv()
        use(z + 4, r, False)
        send_sums(r)
        if r > 0:
            add_sums(r - 1)
    add_sums(NG - 1)

    for r in range(NG):
        for direction in range(2):
            for step in range(1, 5):
                around(direction, step, r).wait_send()
        for dz in range(8):
            across(dz, r).wait_send()
        for dx in range(1, 4):
            exchange(dx, r).wait_send()


def project(a, w):
    bf, f32 = jnp.bfloat16, jnp.float32
    vm = pltpu.VMEM
    dma = pltpu.SemaphoreType.DMA
    rows_g = 512 // NG
    return pl.pallas_call(
        project_kernel,
        out_shape=jax.ShapeDtypeStruct((2, 8, 32, 256), bf),
        in_specs=[pl.BlockSpec(memory_space=pltpu.VMEM), pl.BlockSpec(memory_space=pl.ANY)],
        out_specs=pl.BlockSpec(memory_space=pltpu.VMEM),
        scratch_shapes=[
            vm((4096, 1024), bf),
            vm((2, 8, 4, 8, 32, 128), bf),
            vm((NG, rows_g, 1024), f32),
            vm((3, NG, rows_g, 256), bf),
            vm((3, NG, rows_g, 256), bf),
            dma((2,)),
            dma((2, 4, NG)), dma((2, 4, NG)),
            dma((8, NG)), dma((8, NG)),
            dma((3, NG)), dma((3, NG)),
        ],
        compiler_params=pltpu.CompilerParams(
            collective_id=2, has_side_effects=True, vmem_limit_bytes=48 * MIB
        ),
        name="project",
    )(a, w)


def body(prefill_kv, page_match, queries, new_kv, slot_request, page_table, context_len, out_weight):
    bf = jnp.bfloat16
    q = queries.reshape(8, 2, 2, 8, 4, HD).transpose(3, 4, 1, 2, 0, 5).reshape(8, 8, 16, HD)
    new = new_kv.transpose(3, 1, 2, 0, 4).reshape(2, 1, 8, 8, HD)
    new = jnp.broadcast_to(new, (2, 4, 8, 8, HD)).reshape(8, 8, 8, HD)
    request = slot_request.reshape(8, 1)
    ids = jnp.concatenate(
        [jnp.broadcast_to(request // 8, (8, 64)), jnp.broadcast_to(request % 8, (8, 64))], axis=1
    ).astype(bf)
    ids = jnp.broadcast_to(ids[None, None], (8, 8, 8, HD))
    qx = jnp.concatenate([q, new, ids], axis=2)
    lengths = context_len.reshape(1, 8)
    ti = jnp.concatenate(
        [page_table.reshape(8, MAXP).T, lengths // PAGE, lengths % PAGE, jnp.zeros((14, 8), jnp.int32)], axis=0
    )
    ti = jnp.tile(ti, (1, 16)).astype(bf)
    mm = jnp.pad(page_match.reshape(1, 64), ((0, 0), (0, 64)))
    a = attend(qx, ti, mm, prefill_kv)
    out = project(a, out_weight)
    out = out.reshape(2, 8, 4, 8, 256).transpose(1, 0, 3, 2, 4)
    return out.reshape(128, 1, STEPS, 256)


def solution(mesh):
    in_specs = (
        P(("pre", "grp"), None, "kv", None, None),
        P(("pre", "grp"), None, None),
        P(("pre", "grp"), None, "kv", None),
        P(("pre", "grp"), None, None, "kv", None),
        P("pre", "grp"),
        P("pre", "grp", None),
        P("pre", "grp"),
        P("kv", "pre"),
    )
    out_specs = P(None, "grp", None, ("pre", "kv"))
    return jax.shard_map(body, mesh=mesh, in_specs=in_specs, out_specs=out_specs, check_vma=False)
```

```python
import functools

import jax
import jax.numpy as jnp
from jax import lax
from jax.experimental import pallas as pl
from jax.experimental.pallas import tpu as pltpu
from jax.sharding import PartitionSpec as P

MESH = pl.DeviceIdType.MESH
HD = 128
PAGE = 64
STEPS = 4
MAXP = 32
NZ = 8
NM = 8
LOG2E = 1.4426950408889634
SCALE = LOG2E / HD**0.5
DEAD = -float(2**100)
MIB = 1 << 20
NG = 4
GROUPS = ((0, 1), (1, 2), (3, 2), (5, 3))
PAIRS = (0, 3, 1, 2)
NT = (((1,), (1,)), ((), ()))


def here():
    p = lax.axis_index("pre")
    return p // 2, p % 2, lax.axis_index("grp")


def dev(z, c, y):
    return {"pre": z * 2 + c, "grp": y}


def dev_zm(z, m):
    return dev(z, m // 4, m % 4)


def wrap(a, n):
    return lax.rem(a + 2 * n, n)


def remote(src, dst, ssem, rsem, device):
    return pltpu.make_async_remote_copy(
        src_ref=src, dst_ref=dst, send_sem=ssem, recv_sem=rsem, device_id=device, device_id_type=MESH
    )


def rank(rel):
    return 0 if rel == 0 else 2 * rel - 1 if rel <= 4 else 2 * (8 - rel)


def merge(a, b):
    acc_a, m_a, l_a = a
    acc_b, m_b, l_b = b
    top = jnp.maximum(m_a, m_b)
    fa = jnp.exp2(m_a - top)
    fb = jnp.exp2(m_b - top)
    return acc_a * fa + acc_b * fb, top, l_a * fa + l_b * fb


def iota(shape, dim):
    return lax.broadcasted_iota(jnp.int32, shape, dim)


def one_hot(mask):
    return mask.astype(jnp.float32).astype(jnp.bfloat16)


def kernel(
    q_in, new_in, table_in, len_in, req_in, match_in, pg_hbm, w_hbm, out,
    qx, i1, qg, ng, nh, mmv, mms, pages0, pages1, pages2, pages3, kd, vt, bi, rs_out, rs_in, w, g, acc, xs, xr,
    loc, sps, spr, nhs, nhr, mss, msr, qys, qyr, qfs, qfr, qcs, qcr, ys, yr, ys2, yr2, cs, cr, as_, ar, rss, rsr,
    zs, zr, ks, kr, xss, xsr,
):
    z, c, y = here()
    kx = lax.axis_index("kv")
    me_m = c * 4 + y
    z_up, z_dn = wrap(z + 1, 8), wrap(z - 1, 8)
    y_up, y_dn = wrap(y + 1, 4), wrap(y - 1, 4)

    bar = pltpu.get_barrier_semaphore()
    for k in range(1, 8):
        pl.semaphore_signal(bar, inc=1, device_id=dev(wrap(z + k, 8), c, y), device_id_type=MESH)
        pl.semaphore_signal(bar, inc=1, device_id=dev_zm(z, wrap(me_m + k, 8)), device_id_type=MESH)
    for dx in range(1, 4):
        pl.semaphore_signal(bar, inc=1, device_id={"kv": wrap(kx + dx, 4)}, device_id_type=MESH)
    pages_at = (pages0, pages1, pages2, pages3)
    own_pages = pltpu.make_async_copy(pg_hbm, pages0.at[c], loc.at[0])
    own_pages.start()
    w_copy = pltpu.make_async_copy(w_hbm, w, loc.at[2])
    w_copy.start()

    row = iota((128, 1024), 0)
    origin = (row % 8) * 128 + ((row // 8) % 4) * 32 + row // 32 - iota((128, 1024), 1)

    def arrange(zj, carry):
        hot = one_hot(origin == -4 * zj)
        rows = jnp.dot(hot, q_in[...].reshape(1024, 128), preferred_element_type=jnp.float32)
        qx[zj, 0:8] = rows.astype(jnp.bfloat16).reshape(8, 16, 128)
        return carry

    lax.fori_loop(0, 8, arrange, 0)
    row = iota((128, 128), 0)
    lane = iota((128, 128), 1)
    origin = (row % 8) * 16 + ((row // 8) % 4) * 4 + ((row // 32) % 2) * 2 + row // 64
    new = jnp.dot(one_hot(origin == lane), new_in[...], preferred_element_type=jnp.float32).astype(jnp.bfloat16)
    lane8 = iota((8, 128), 1)
    facts = jnp.concatenate([table_in[...], jnp.zeros((8, 128 - MAXP), jnp.int32)], axis=1)

    def to_column(ref):
        line = jnp.concatenate([ref[...], jnp.zeros((1, 120), jnp.int32)], axis=1)
        line = jnp.where(lane8 == iota((8, 128), 0), jnp.broadcast_to(line, (8, 128)), 0)
        return jnp.broadcast_to(jnp.sum(line, axis=1, keepdims=True), (8, 128))

    length = to_column(len_in)
    request = to_column(req_in)
    for n, values in enumerate((length >> 6, length & 63, request >> 3, request & 7)):
        facts = jnp.where(lane8 == MAXP + n, values, facts)
    facts = facts.astype(jnp.float32)
    facts = jnp.concatenate([facts, facts], axis=0).astype(jnp.bfloat16)
    for zj in range(8):
        qx[zj, 8] = new[16 * zj : 16 * zj + 16]
        qx[zj, 9] = facts
    i1[me_m, 0] = qx[z]
    mmv[me_m] = jnp.concatenate([match_in[...], jnp.zeros((1, 64), jnp.int32)], axis=1)
    pl.semaphore_wait(bar, 17)

    def spread(kz):
        zj = wrap(z + kz, 8)
        return remote(qx.at[zj], i1.at[me_m, rank(8 - kz)], sps.at[kz], spr.at[rank(8 - kz)], dev(zj, c, y))

    def match_copy(km):
        return remote(mmv.at[me_m], mmv.at[me_m], mss.at[km], msr.at[km], dev_zm(z, wrap(me_m + km, 8)))

    def m_of(cc, yy):
        return cc * 4 + wrap(yy, 4)

    def y_dev(direction):
        return dev(z, c, y_up if direction == 0 else y_dn)

    def m_behind(direction):
        return m_of(c, y - 1 if direction == 0 else y + 1)

    def part(m, gi, tile, tiles):
        lo, n = GROUPS[gi]
        return i1.at[m, pl.ds(lo, n), pl.ds(tile, tiles)]

    def q_y(direction, gi):
        ref = part(me_m, gi, 0, 9)
        return remote(ref, ref, qys.at[direction, gi], qyr.at[direction, gi], y_dev(direction))

    def q_far(direction, gi):
        ref = part(m_behind(direction), gi, 5 * direction, 5 - direction)
        return remote(ref, ref, qfs.at[direction, gi], qfr.at[direction, gi], y_dev(direction))

    def q_core(dy, gi):
        ref = part(m_of(c, y + dy), gi, 0, 9)
        return remote(ref, ref, qcs.at[dy, gi], qcr.at[dy, gi], dev(z, 1 - c, y))

    behind = (3, 1)

    def quarter(dy, q):
        return pages_at[dy].at[c, pl.ds(4 * q, 4)]

    def y_copy(direction, q):
        return remote(
            quarter(0, q), quarter(behind[direction], q), ys.at[direction, q], yr.at[direction, q], y_dev(direction)
        )

    def y_far(direction, q):
        return remote(quarter(behind[direction], q), quarter(2, q), ys2.at[q], yr2.at[q], y_dev(direction))

    def core_copy(dy, q):
        return remote(quarter(dy, q), quarter(dy, q), cs.at[dy, q], cr.at[dy, q], dev(z, 1 - c, y))

    order = ((0, 1, 2, 3), (2, 3, 0, 1))

    for kz in (1, 7, 2, 6, 3, 5, 4):
        spread(kz).start()
    for km in range(1, 8):
        match_copy(km).start()

    def send_group(gi):
        q_y(0, gi).start()
        q_y(1, gi).start()
        q_core(0, gi).start()

    def send_pages(n):
        for direction in range(2):
            y_copy(direction, order[direction][n]).start()

    def forward_pages(n):
        for direction in range(2):
            q = order[direction][n]
            y_copy(direction, q).wait_recv()
            if n < 2:
                y_far(direction, q).start()
            core_copy(behind[direction], q).start()

    send_group(0)
    own_pages.wait()
    send_pages(0)
    for gi in range(1, 4):
        lo, n = GROUPS[gi]
        for rk in range(lo, lo + n):
            kz = [k for k in range(1, 8) if rank(8 - k) == rk][0]
            spread(kz).wait_recv()
        send_group(gi)
    for gi in range(4):
        for direction in range(2):
            q_y(direction, gi).wait_recv()
            q_far(direction, gi).start()
            q_core(behind[direction], gi).start()
    send_pages(1)
    forward_pages(0)
    send_pages(2)
    send_pages(3)
    for q in range(4):
        core_copy(0, q).start()

    def biases(d, carry):
        rows = i1[me_m, from_plane(d), 9].astype(jnp.float32)
        rows = jnp.transpose(jnp.concatenate([rows] * 8, axis=0))
        pages = rows[0:32]
        whole = rows[32:33]
        rest = rows[33:34]
        slot = iota((32, 128), 0).astype(jnp.float32)
        before = (slot < whole).astype(jnp.float32)
        at = (slot == whole).astype(jnp.float32)
        within = iota((PAGE, 128), 0).astype(jnp.float32) < rest
        for m in range(8):
            number = z * 8 + m_of(m % 2, y + PAIRS[m // 2])
            same = (pages == number.astype(jnp.float32)).astype(jnp.float32)
            full = jnp.sum(same * before, axis=0, keepdims=True)
            more = full + jnp.sum(same * at, axis=0, keepdims=True)
            low = jnp.where(full > 0.0, jnp.log(jnp.maximum(full, 1.0)) * LOG2E, DEAD)
            high = jnp.where(more > 0.0, jnp.log(jnp.maximum(more, 1.0)) * LOG2E, DEAD)
            bi[d, m * PAGE : (m + 1) * PAGE, :] = jnp.where(within, high, low)
        return carry

    def from_plane(d):
        rel = wrap(d - z, 8)
        return jnp.where(rel == 0, 0, jnp.where(rel <= 4, 2 * rel - 1, 2 * (8 - rel)))

    for gi in range(4):
        for direction in range(2):
            q_far(direction, gi).wait_recv()
        q_core(2, gi).start()
    for gi in range(4):
        for dy in (0, 1, 3, 2):
            q_core(dy, gi).wait_recv()

    facts = jnp.concatenate([i1[me_m, from_plane(d), 9] for d in range(8)], axis=0).astype(jnp.float32)
    source = facts[:, 34:35].astype(jnp.int32)
    within = facts[:, 35:36].astype(jnp.int32)
    rel = ((source >> 3) - z + 8) & 7
    ranked = jnp.where(rel == 0, 0, jnp.where(rel <= 4, 2 * rel - 1, 2 * (8 - rel)))
    column = ((source & 7) * 8 + ranked) * 16 + within
    column = jnp.broadcast_to(column, (128, 1024)) + (iota((128, 1024), 0) & 8)
    hot = one_hot(column == iota((128, 1024), 1))
    for fp in range(9):
        rows = jnp.dot(
            hot, i1[:, :, fp].reshape(1024, 128), preferred_element_type=jnp.float32
        ).astype(jnp.bfloat16).reshape(8, 16, 128)
        if fp < 8:
            qg[z, fp] = rows
        else:
            ng[...] = rows

    def around(direction, step):
        sign = 1 if direction == 0 else -1
        o = wrap(z - sign * (step - 1), 8)
        ref = qg.at[o] if step < 4 else qg.at[o, :, pl.ds(4 * direction, 4)]
        target = dev(z_up if direction == 0 else z_dn, c, y)
        return remote(ref, ref, as_.at[direction, step - 1], ar.at[direction, step - 1], target)

    def pass_on(step):
        for direction in range(2):
            around(direction, step).wait_recv()
            around(direction, step + 1).start()

    for direction in range(2):
        around(direction, 1).start()

    def new_copy(kz):
        zj = wrap(z + kz, 8)
        return remote(ng.at[zj], nh.at[z], nhs.at[kz], nhr.at[kz], dev(zj, c, y))

    for kz in range(1, 8):
        new_copy(kz).start()
    nh[z] = ng[z]

    lax.fori_loop(0, 8, biases, 0)
    eye = one_hot(row == lane)

    def select_pages(pair):
        dy = PAIRS[pair]

        def one(d, carry):
            picks = [mms[m_of(k, y + dy), 0, d * 8 + me_m] for k in range(2)]
            for h in range(2):
                values = []
                for k in range(2):
                    m = 2 * pair + k
                    kd[d, h, m * PAGE : (m + 1) * PAGE, :] = pages_at[dy][k, picks[k], 0, h]
                    values.append(pages_at[dy][k, picks[k], 1, h])
                turned = lax.dot_general(
                    eye, jnp.concatenate(values, axis=0), NT, preferred_element_type=jnp.float32
                )
                vt[d, h, :, pair * 128 : (pair + 1) * 128] = turned.astype(jnp.bfloat16)
            return carry

        lax.fori_loop(0, 8, one, 0)

    def wait_cores(dy):
        for q in range(4):
            core_copy(dy, q).wait_recv()

    for km in range(1, 8):
        match_copy(km).wait_recv()
    to_smem = pltpu.make_async_copy(mmv, mms, loc.at[1])
    to_smem.start()
    forward_pages(1)
    to_smem.wait()
    wait_cores(0)
    select_pages(0)
    pass_on(1)
    forward_pages(2)
    pass_on(2)
    forward_pages(3)
    wait_cores(3)
    select_pages(1)
    wait_cores(1)
    select_pages(2)
    pass_on(3)
    for q in range(4):
        y_far(0 if q < 2 else 1, q).wait_recv()
        core_copy(2, q).start()
    wait_cores(2)
    select_pages(3)
    for direction in range(2):
        around(direction, 4).wait_recv()
    for kz in range(1, 8):
        new_copy(kz).wait_recv()

    def unit(o, d):
        h = o // 4
        q = qg[o, :, d].reshape(128, 128)
        s = lax.dot_general(kd[d, h], q, NT, preferred_element_type=jnp.float32)
        s = s * SCALE + bi[d]
        top = jnp.max(s, axis=0, keepdims=True)
        wt = jnp.exp2(s - top)
        total = jnp.sum(wt, axis=0, keepdims=True)
        part = jnp.dot(vt[d, h], wt.astype(jnp.bfloat16), preferred_element_type=jnp.float32)
        return part, top, total

    nrow = iota((32, 128), 0)
    nlane = iota((32, 128), 1)
    valid = (nrow % 8 == nlane % 8) & (nrow // 8 <= (nlane // 8) % 4)

    def fresh(o):
        h = o // 4
        q = qg[o, :, z].reshape(128, 128)
        keys = nh[pl.ds(4 * h, 2)].reshape(32, 128)
        vals = nh[pl.ds(4 * h + 2, 2)].reshape(32, 128)
        s = lax.dot_general(keys, q, NT, preferred_element_type=jnp.float32) * SCALE
        s = jnp.where(valid, s, DEAD)
        top = jnp.max(s, axis=0, keepdims=True)
        wt = jnp.exp2(s - top)
        total = jnp.sum(wt, axis=0, keepdims=True)
        turned = lax.dot_general(eye, vals, NT, preferred_element_type=jnp.float32).astype(jnp.bfloat16)
        part = jnp.dot(turned, wt.astype(jnp.bfloat16), preferred_element_type=jnp.float32)
        return part, top, total

    def units(o, half):
        num, top, total = fresh(o)
        return [
            merge(unit(o, d), (num, jnp.where(z == d, top, DEAD), total)) for d in range(4 * half, 4 * half + 4)
        ]

    row16 = iota((16, 128), 0)

    def back(direction, k, half):
        target = dev(z_dn if direction == 0 else z_up, c, y)
        return remote(
            rs_out.at[direction, k - 1, half], rs_in.at[direction, k - 1, half],
            rss.at[direction, k - 1, half], rsr.at[direction, k - 1, half], target,
        )

    def unpack(direction, k, half):
        st = rs_in[direction, k - 1, half, 512:528, :].astype(jnp.float32)
        return [
            (
                rs_in[direction, k - 1, half, 128 * i : 128 * i + 128, :].astype(jnp.float32),
                st[3 * i : 3 * i + 1],
                st[3 * i + 1 : 3 * i + 2] + st[3 * i + 2 : 3 * i + 3],
            )
            for i in range(4)
        ]

    def give(direction, k, half, o, merged):
        parts = units(o, half)
        if merged:
            back(direction, k + 1, half).wait_recv()
            parts = [merge(a, b) for a, b in zip(parts, unpack(direction, k + 1, half))]
        stats = jnp.zeros((16, 128), jnp.float32)
        for i, (num, top, total) in enumerate(parts):
            top_b = top.astype(jnp.bfloat16).astype(jnp.float32)
            shift = jnp.exp2(top - top_b)
            top, total = top_b, total * shift
            rs_out[direction, k - 1, half, 128 * i : 128 * i + 128, :] = (num * shift).astype(jnp.bfloat16)
            total_hi = total.astype(jnp.bfloat16).astype(jnp.float32)
            for n, values in enumerate((top, total_hi, total - total_hi)):
                stats = jnp.where(row16 == 3 * i + n, values, stats)
        rs_out[direction, k - 1, half, 512:528, :] = stats.astype(jnp.bfloat16)
        back(direction, k, half).start()

    for direction in range(2):
        give(direction, 4, direction, wrap(z + 4, 8), False)
    for k in (3, 2, 1):
        for n in range(2):
            for direction in range(2):
                half = direction if n == 0 else 1 - direction
                give(direction, k, half, wrap(z - k if direction == 0 else z + k, 8), k < 3 or n == 0)

    ds = 8 // NG

    def rows_of(ref, r):
        return ref.at[:, pl.ds(r * ds, ds)]

    def gather(direction, step, r):
        sign = 1 if direction == 0 else -1
        o = wrap(z - sign * (step - 1), 8)
        ref = g.at[c, o]
        ref = rows_of(ref, r) if step < 4 else ref.at[pl.ds(2 * direction, 2), pl.ds(r * ds, ds)]
        target = dev(z_up if direction == 0 else z_dn, c, y)
        return remote(ref, ref, zs.at[direction, step - 1, r], zr.at[direction, step - 1, r], target)

    def across(dz, r):
        ref = rows_of(g.at[c, wrap(z + dz, 8)], r)
        return remote(ref, ref, ks.at[dz, r], kr.at[dz, r], dev(z, 1 - c, y))

    parts = units(z, 0) + units(z, 1)
    for half in range(2):
        for direction in range(2):
            back(direction, 1, half).wait_recv()
        below, above = unpack(0, 1, half), unpack(1, 1, half)
        for i in range(4):
            d = 4 * half + i
            num, _, total = merge(merge(parts[d], below[i]), above[i])
            rows = jnp.transpose(num / total).astype(jnp.bfloat16)
            for h in range(4):
                g[c, z, h, d] = rows[h * 32 : (h + 1) * 32]
            if (d + 1) % ds == 0:
                r = d // ds
                for direction in range(2):
                    gather(direction, 1, r).start()
                across(0, r).start()

    w_copy.wait()

    def exchange(dx, r):
        return remote(
            xs.at[dx - 1, r], xr.at[dx - 1, r], xss.at[dx - 1, r], xsr.at[dx - 1, r], {"kv": wrap(kx + dx, 4)}
        )

    def use(o, r, first):
        o = wrap(o, 8)
        block = g[:, o, :, pl.ds(r * ds, ds)].reshape(2, 4, ds * 32, 128)
        left = jnp.concatenate(
            [jnp.concatenate([block[cc, h] for h in range(4)], axis=1) for cc in range(2)], axis=0
        )
        step = jnp.dot(
            left, w[pl.ds(pl.multiple_of(o * 512, 512), 512), :], preferred_element_type=jnp.float32
        )
        if first:
            acc[r] = step
        else:
            acc[r] += step

    def send_sums(r):
        for dx in range(1, 4):
            kk = wrap(kx + dx, 4)
            xs[dx - 1, r] = acc[r, :, pl.ds(pl.multiple_of(kk * 256, 256), 256)].astype(jnp.bfloat16)
            exchange(dx, r).start()

    def add_sums(r):
        total = acc[r, :, pl.ds(pl.multiple_of(kx * 256, 256), 256)]
        for dx in range(1, 4):
            exchange(dx, r).wait_recv()
            total = total + xr[dx - 1, r].astype(jnp.float32)
        out[:, pl.ds(r * ds, ds)] = total.astype(jnp.bfloat16).reshape(2, ds, 32, 256)

    for r in range(NG):
        across(0, r).wait_recv()
        use(z, r, True)
    waiting = []

    def settle(left):
        while len(waiting) > left:
            dz, r = waiting.pop(0)
            across(dz % 8, r).wait_recv()
            use(z + dz, r, False)
            if dz == 4:
                send_sums(r)
                if r > 0:
                    add_sums(r - 1)

    for step in range(1, 4):
        for r in range(NG):
            for direction in range(2):
                dz = -step if direction == 0 else step
                gather(direction, step, r).wait_recv()
                gather(direction, step + 1, r).start()
                across(dz % 8, r).start()
                waiting.append((dz, r))
            settle(2)
    for r in range(NG):
        for direction in range(2):
            gather(direction, 4, r).wait_recv()
        across(4, r).start()
        waiting.append((4, r))
        settle(1)
    settle(0)
    add_sums(NG - 1)

    for k in range(1, 8):
        spread(k).wait_send()
        match_copy(k).wait_send()
        new_copy(k).wait_send()
    for n in range(4):
        for direction in range(2):
            q_y(direction, n).wait_send()
            q_far(direction, n).wait_send()
            y_copy(direction, n).wait_send()
        y_far(0 if n < 2 else 1, n).wait_send()
        for dy in range(4):
            q_core(dy, n).wait_send()
            core_copy(dy, n).wait_send()
    for direction in range(2):
        for step in range(1, 5):
            around(direction, step).wait_send()
        for k in (1, 2, 3):
            for half in range(2):
                back(direction, k, half).wait_send()
        back(direction, 4, direction).wait_send()
    for r in range(NG):
        for direction in range(2):
            for step in range(1, 5):
                gather(direction, step, r).wait_send()
        for dz in range(8):
            across(dz, r).wait_send()
        for dx in range(1, 4):
            exchange(dx, r).wait_send()


def decode(*args):
    bf, f32 = jnp.bfloat16, jnp.float32
    vm = pltpu.VMEM
    dma = pltpu.SemaphoreType.DMA
    rows_g = 512 // NG
    return pl.pallas_call(
        kernel,
        out_shape=jax.ShapeDtypeStruct((2, 8, 32, 256), bf),
        in_specs=[pl.BlockSpec(memory_space=pltpu.VMEM)] * 6 + [pl.BlockSpec(memory_space=pl.ANY)] * 2,
        out_specs=pl.BlockSpec(memory_space=pltpu.VMEM),
        scratch_shapes=[
            vm((8, 10, 16, 128), bf),
            vm((8, 8, 10, 16, 128), bf),
            vm((8, 8, 8, 16, 128), bf),
            vm((8, 16, 128), bf),
            vm((8, 16, 128), bf),
            vm((8, 1, 128), jnp.int32),
            pltpu.SMEM((8, 1, 128), jnp.int32),
            vm((2, 16, 2, 2, PAGE, 128), bf),
            vm((2, 16, 2, 2, PAGE, 128), bf),
            vm((2, 16, 2, 2, PAGE, 128), bf),
            vm((2, 16, 2, 2, PAGE, 128), bf),
            vm((8, 2, 512, 128), bf),
            vm((8, 2, 128, 512), bf),
            vm((8, 512, 128), f32),
            vm((2, 4, 2, 528, 128), bf),
            vm((2, 4, 2, 528, 128), bf),
            vm((4096, 1024), bf),
            vm((2, 8, 4, 8, 32, 128), bf),
            vm((NG, rows_g, 1024), f32),
            vm((3, NG, rows_g, 256), bf),
            vm((3, NG, rows_g, 256), bf),
            dma((3,)),
            dma((8,)), dma((8,)),
            dma((8,)), dma((8,)),
            dma((8,)), dma((8,)),
            dma((2, 4)), dma((2, 4)),
            dma((2, 4)), dma((2, 4)),
            dma((4, 4)), dma((4, 4)),
            dma((2, 4)), dma((2, 4)),
            dma((4,)), dma((4,)),
            dma((4, 4)), dma((4, 4)),
            dma((2, 4)), dma((2, 4)),
            dma((2, 4, 2)), dma((2, 4, 2)),
            dma((2, 4, NG)), dma((2, 4, NG)),
            dma((8, NG)), dma((8, NG)),
            dma((3, NG)), dma((3, NG)),
        ],
        compiler_params=pltpu.CompilerParams(
            collective_id=1, has_side_effects=True, vmem_limit_bytes=60 * MIB
        ),
        name="decode",
    )(*args)


def body(prefill_kv, page_match, queries, new_kv, slot_request, page_table, context_len, out_weight):
    out = decode(
        queries, new_kv.reshape(128, HD), page_table.reshape(8, MAXP), context_len.reshape(1, 8),
        slot_request.reshape(1, 8), page_match.reshape(1, 64), prefill_kv, out_weight,
    )
    out = out.reshape(2, 8, 4, 8, 256).transpose(1, 0, 3, 2, 4)
    return out.reshape(128, 1, STEPS, 256)


def solution(mesh):
    in_specs = (
        P(("pre", "grp"), None, "kv", None, None),
        P(("pre", "grp"), None, None),
        P(("pre", "grp"), None, "kv", None),
        P(("pre", "grp"), None, None, "kv", None),
        P("pre", "grp"),
        P("pre", "grp", None),
        P("pre", "grp"),
        P("kv", "pre"),
    )
    out_specs = P(None, "grp", None, ("pre", "kv"))
    return jax.shard_map(body, mesh=mesh, in_specs=in_specs, out_specs=out_specs, check_vma=False)
```

```python
import functools

import jax
import jax.numpy as jnp
from jax import lax
from jax.experimental import pallas as pl
from jax.experimental.pallas import tpu as pltpu
from jax.sharding import PartitionSpec as P

MESH = pl.DeviceIdType.MESH
HD = 128
PAGE = 64
STEPS = 4
MAXP = 32
NZ = 8
NM = 8
LOG2E = 1.4426950408889634
SCALE = LOG2E / HD**0.5
DEAD = -float(2**100)
MIB = 1 << 20
NG = 4
GROUPS = ((0, 2), (2, 2), (4, 2), (6, 2))
PAIRS = (0, 3, 1, 2)
CHUNKS = (((0, 2), (2, 4), (6, 2), (8, 8)), ((8, 2), (10, 4), (14, 2), (0, 8)))
NT = (((1,), (1,)), ((), ()))


def here():
    p = lax.axis_index("pre")
    return p // 2, p % 2, lax.axis_index("grp")


def dev(z, c, y):
    return {"pre": z * 2 + c, "grp": y}


def dev_zm(z, m):
    return dev(z, m // 4, m % 4)


def wrap(a, n):
    return lax.rem(a + 2 * n, n)


def remote(src, dst, ssem, rsem, device):
    return pltpu.make_async_remote_copy(
        src_ref=src, dst_ref=dst, send_sem=ssem, recv_sem=rsem, device_id=device, device_id_type=MESH
    )


def rank(rel):
    return 0 if rel == 0 else 1 if rel == 4 else 8 - 2 * rel if rel < 4 else 2 * rel - 7


def merge(a, b):
    acc_a, m_a, l_a = a
    acc_b, m_b, l_b = b
    top = jnp.maximum(m_a, m_b)
    fa = jnp.exp2(m_a - top)
    fb = jnp.exp2(m_b - top)
    return acc_a * fa + acc_b * fb, top, l_a * fa + l_b * fb


def ranks(rel):
    side = jnp.where(rel < 4, 8 - 2 * rel, 2 * rel - 7)
    return jnp.where(rel == 0, 0, jnp.where(rel == 4, 1, side))


def iota(shape, dim):
    return lax.broadcasted_iota(jnp.int32, shape, dim)


def one_hot(mask):
    return mask.astype(jnp.float32).astype(jnp.bfloat16)


def kernel(
    q_hbm, new_hbm, table_hbm, len_hbm, req_hbm, match_hbm, pg_hbm, w_hbm, out,
    q_in, new_in, table_in, len_in, req_in, match_in,
    qf, qx, i1, qg, ng, nh, mmv, mms, pages0, pages1, pages2, pages3, kd, vt, bi, rs_out, rs_in, w, g, acc, xs, xr,
    loc, sps, spr, nhs, nhr, mss, msr, qys, qyr, qfs, qfr, qcs, qcr, ys, yr, ys2, yr2, cs, cr, as_, ar, rss, rsr,
    zs, zr, ks, kr, xss, xsr,
):
    z, c, y = here()
    kx = lax.axis_index("kv")
    me_m = c * 4 + y
    z_up, z_dn = wrap(z + 1, 8), wrap(z - 1, 8)
    y_up, y_dn = wrap(y + 1, 4), wrap(y - 1, 4)

    loads = [
        pltpu.make_async_copy(src, dst, loc.at[3 + n])
        for n, (src, dst) in enumerate(
            (
                (q_hbm, q_in), (new_hbm, new_in), (table_hbm, table_in), (len_hbm, len_in), (req_hbm, req_in),
                (match_hbm, match_in),
            )
        )
    ]
    for load in loads:
        load.start()
    bar = pltpu.get_barrier_semaphore()
    for k in range(1, 8):
        pl.semaphore_signal(bar, inc=1, device_id=dev(wrap(z + k, 8), c, y), device_id_type=MESH)
        pl.semaphore_signal(bar, inc=1, device_id=dev_zm(z, wrap(me_m + k, 8)), device_id_type=MESH)
    for dx in range(1, 4):
        pl.semaphore_signal(bar, inc=1, device_id={"kv": wrap(kx + dx, 4)}, device_id_type=MESH)
    pages_at = (pages0, pages1, pages2, pages3)
    own_pages = pltpu.make_async_copy(pg_hbm, pages0.at[c], loc.at[0])
    own_pages.start()
    w_copy = pltpu.make_async_copy(w_hbm, w, loc.at[2])
    w_copy.start()

    for load in loads:
        load.wait()
    qf[...] = q_in[...].reshape(1024, 128).astype(jnp.float32)

    def arrange(zj, carry):
        for tile in range(8):
            h, t = tile // 2, 2 * (tile % 2)
            rows = [qf[pl.ds((t + k) * 32 + 4 * zj + h, 8, stride=128), :] for k in range(2)]
            qx[zj, tile] = jnp.concatenate(rows, axis=0).astype(jnp.bfloat16)
        return carry

    lax.fori_loop(0, 8, arrange, 0)
    row = iota((128, 128), 0)
    lane = iota((128, 128), 1)
    origin = (row % 8) * 16 + ((row // 8) % 4) * 4 + ((row // 32) % 2) * 2 + row // 64
    new = jnp.dot(one_hot(origin == lane), new_in[...], preferred_element_type=jnp.float32).astype(jnp.bfloat16)
    lane8 = iota((8, 128), 1)
    facts = jnp.concatenate([table_in[...], jnp.zeros((8, 128 - MAXP), jnp.int32)], axis=1)

    def to_column(ref):
        line = jnp.concatenate([ref[...], jnp.zeros((1, 120), jnp.int32)], axis=1)
        line = jnp.where(lane8 == iota((8, 128), 0), jnp.broadcast_to(line, (8, 128)), 0)
        return jnp.broadcast_to(jnp.sum(line, axis=1, keepdims=True), (8, 128))

    length = to_column(len_in)
    request = to_column(req_in)
    for n, values in enumerate((length >> 6, length & 63, request >> 3, request & 7)):
        facts = jnp.where(lane8 == MAXP + n, values, facts)
    facts = facts.astype(jnp.float32)
    facts = jnp.concatenate([facts, facts], axis=0).astype(jnp.bfloat16)
    for zj in range(8):
        qx[zj, 8] = new[16 * zj : 16 * zj + 16]
        qx[zj, 9] = facts
    i1[me_m, 0] = qx[z]
    mmv[me_m] = jnp.concatenate([match_in[...], jnp.zeros((1, 64), jnp.int32)], axis=1)
    pl.semaphore_wait(bar, 17)

    def spread(kz):
        zj = wrap(z + kz, 8)
        return remote(qx.at[zj], i1.at[me_m, rank(8 - kz)], sps.at[kz], spr.at[rank(8 - kz)], dev(zj, c, y))

    def match_copy(km):
        return remote(mmv.at[me_m], mmv.at[me_m], mss.at[km], msr.at[km], dev_zm(z, wrap(me_m + km, 8)))

    def m_of(cc, yy):
        return cc * 4 + wrap(yy, 4)

    def y_dev(direction):
        return dev(z, c, y_up if direction == 0 else y_dn)

    def m_behind(direction):
        return m_of(c, y - 1 if direction == 0 else y + 1)

    def part(m, gi, tile, tiles):
        lo, n = GROUPS[gi]
        return i1.at[m, pl.ds(lo, n), pl.ds(tile, tiles)]

    def q_y(direction, gi):
        ref = part(me_m, gi, 0, 9)
        return remote(ref, ref, qys.at[direction, gi], qyr.at[direction, gi], y_dev(direction))

    def q_far(direction, gi):
        ref = part(m_behind(direction), gi, 5 * direction, 5 - direction)
        return remote(ref, ref, qfs.at[direction, gi], qfr.at[direction, gi], y_dev(direction))

    def q_core(dy, gi):
        ref = part(m_of(c, y + dy), gi, 0, 9)
        return remote(ref, ref, qcs.at[dy, gi], qcr.at[dy, gi], dev(z, 1 - c, y))

    behind = (3, 1)

    def chunk(dy, lo, n):
        return pages_at[dy].at[c, pl.ds(lo, n)]

    def y_copy(direction, n):
        lo, count = CHUNKS[direction][n]
        return remote(
            chunk(0, lo, count), chunk(behind[direction], lo, count),
            ys.at[direction, n], yr.at[direction, n], y_dev(direction),
        )

    def y_far(direction, n):
        lo, count = CHUNKS[direction][n]
        return remote(
            chunk(behind[direction], lo, count), chunk(2, lo, count),
            ys2.at[direction, n], yr2.at[direction, n], y_dev(direction),
        )

    def core_copy(dy, n):
        lo, count = ((CHUNKS[0][:3] + CHUNKS[1][:3]) if dy == 2 else CHUNKS[1 if dy == 1 else 0])[n]
        return remote(chunk(dy, lo, count), chunk(dy, lo, count), cs.at[dy, n], cr.at[dy, n], dev(z, 1 - c, y))

    for kz in (4, 3, 5, 2, 6, 1, 7):
        spread(kz).start()
    for km in range(1, 8):
        match_copy(km).start()

    def send_group(gi):
        q_y(0, gi).start()
        q_y(1, gi).start()
        q_core(0, gi).start()

    def send_pages(n):
        for direction in range(2):
            y_copy(direction, n).start()

    def forward_pages(n):
        for direction in range(2):
            y_copy(direction, n).wait_recv()
            if n < 3:
                y_far(direction, n).start()
            core_copy(behind[direction], n).start()

    own_pages.wait()
    send_pages(0)
    for gi in range(4):
        lo, n = GROUPS[gi]
        for rk in range(max(lo, 1), lo + n):
            kz = [k for k in range(1, 8) if rank(8 - k) == rk][0]
            spread(kz).wait_recv()
        send_group(gi)
    send_pages(1)
    for gi in range(4):
        for direction in range(2):
            q_y(direction, gi).wait_recv()
            q_far(direction, gi).start()
            q_core(behind[direction], gi).start()
    forward_pages(0)
    send_pages(2)
    send_pages(3)
    for n in range(4):
        core_copy(0, n).start()

    def biases(d, carry):
        rows = i1[me_m, from_plane(d), 9].astype(jnp.float32)
        rows = jnp.transpose(jnp.concatenate([rows] * 8, axis=0))
        pages = rows[0:32]
        whole = rows[32:33]
        rest = rows[33:34]
        slot = iota((32, 128), 0).astype(jnp.float32)
        before = (slot < whole).astype(jnp.float32)
        at = (slot == whole).astype(jnp.float32)
        within = iota((PAGE, 128), 0).astype(jnp.float32) < rest
        for m in range(8):
            number = z * 8 + m_of(m % 2, y + PAIRS[m // 2])
            same = (pages == number.astype(jnp.float32)).astype(jnp.float32)
            full = jnp.sum(same * before, axis=0, keepdims=True)
            more = full + jnp.sum(same * at, axis=0, keepdims=True)
            low = jnp.where(full > 0.0, jnp.log(jnp.maximum(full, 1.0)) * LOG2E, DEAD)
            high = jnp.where(more > 0.0, jnp.log(jnp.maximum(more, 1.0)) * LOG2E, DEAD)
            bi[d, m * PAGE : (m + 1) * PAGE, :] = jnp.where(within, high, low)
        return carry

    def from_plane(d):
        rel = wrap(d - z, 8)
        return ranks(rel)

    for gi in range(4):
        for direction in range(2):
            q_far(direction, gi).wait_recv()
        q_core(2, gi).start()
    for gi in range(4):
        for dy in (0, 1, 3, 2):
            q_core(dy, gi).wait_recv()

    facts = jnp.concatenate([i1[me_m, from_plane(d), 9] for d in range(8)], axis=0).astype(jnp.float32)
    source = facts[:, 34:35].astype(jnp.int32)
    within = facts[:, 35:36].astype(jnp.int32)
    rel = ((source >> 3) - z + 8) & 7
    ranked = ranks(rel)
    column = ((source & 7) * 8 + ranked) * 16 + within
    column = jnp.broadcast_to(column, (128, 1024)) + (iota((128, 1024), 0) & 8)
    hot = one_hot(column == iota((128, 1024), 1))
    for fp in range(9):
        rows = jnp.dot(
            hot, i1[:, :, fp].reshape(1024, 128), preferred_element_type=jnp.float32
        ).astype(jnp.bfloat16).reshape(8, 16, 128)
        if fp < 8:
            qg[z, fp] = rows
        else:
            ng[...] = rows

    def around(direction, step):
        sign = 1 if direction == 0 else -1
        o = wrap(z - sign * (step - 1), 8)
        ref = qg.at[o] if step < 4 else qg.at[o, :, pl.ds(4 * direction, 4)]
        target = dev(z_up if direction == 0 else z_dn, c, y)
        return remote(ref, ref, as_.at[direction, step - 1], ar.at[direction, step - 1], target)

    def pass_on(step):
        for direction in range(2):
            around(direction, step).wait_recv()
            around(direction, step + 1).start()

    for direction in range(2):
        around(direction, 1).start()

    def new_copy(kz):
        zj = wrap(z + kz, 8)
        return remote(ng.at[zj], nh.at[z], nhs.at[kz], nhr.at[kz], dev(zj, c, y))

    for kz in range(1, 8):
        new_copy(kz).start()
    nh[z] = ng[z]

    lax.fori_loop(0, 8, biases, 0)
    eye = one_hot(row == lane)

    def select_pages(pair):
        dy = PAIRS[pair]

        def one(d, carry):
            picks = [mms[m_of(k, y + dy), 0, d * 8 + me_m] for k in range(2)]
            for h in range(2):
                values = []
                for k in range(2):
                    m = 2 * pair + k
                    kd[d, h, m * PAGE : (m + 1) * PAGE, :] = pages_at[dy][k, picks[k], 0, h]
                    values.append(pages_at[dy][k, picks[k], 1, h])
                turned = lax.dot_general(
                    eye, jnp.concatenate(values, axis=0), NT, preferred_element_type=jnp.float32
                )
                vt[d, h, :, pair * 128 : (pair + 1) * 128] = turned.astype(jnp.bfloat16)
            return carry

        lax.fori_loop(0, 8, one, 0)

    def wait_cores(dy):
        for n in range(6 if dy == 2 else 4):
            core_copy(dy, n).wait_recv()

    for km in range(1, 8):
        match_copy(km).wait_recv()
    to_smem = pltpu.make_async_copy(mmv, mms, loc.at[1])
    to_smem.start()
    forward_pages(1)
    to_smem.wait()
    wait_cores(0)
    select_pages(0)
    pass_on(1)
    forward_pages(2)
    pass_on(2)
    forward_pages(3)
    wait_cores(3)
    select_pages(1)
    wait_cores(1)
    select_pages(2)
    pass_on(3)
    for n in range(3):
        for direction in range(2):
            y_far(direction, n).wait_recv()
            core_copy(2, 3 * direction + n).start()
    wait_cores(2)
    select_pages(3)
    for direction in range(2):
        around(direction, 4).wait_recv()
    for kz in range(1, 8):
        new_copy(kz).wait_recv()

    def unit(o, d):
        h = o // 4
        q = qg[o, :, d].reshape(128, 128)
        s = lax.dot_general(kd[d, h], q, NT, preferred_element_type=jnp.float32)
        s = s * SCALE + bi[d]
        top = jnp.max(s, axis=0, keepdims=True)
        wt = jnp.exp2(s - top)
        total = jnp.sum(wt, axis=0, keepdims=True)
        part = jnp.dot(vt[d, h], wt.astype(jnp.bfloat16), preferred_element_type=jnp.float32)
        return part, top, total

    nrow = iota((32, 128), 0)
    nlane = iota((32, 128), 1)
    valid = (nrow % 8 == nlane % 8) & (nrow // 8 <= (nlane // 8) % 4)

    def fresh(o):
        h = o // 4
        q = qg[o, :, z].reshape(128, 128)
        keys = nh[pl.ds(4 * h, 2)].reshape(32, 128)
        vals = nh[pl.ds(4 * h + 2, 2)].reshape(32, 128)
        s = lax.dot_general(keys, q, NT, preferred_element_type=jnp.float32) * SCALE
        s = jnp.where(valid, s, DEAD)
        top = jnp.max(s, axis=0, keepdims=True)
        wt = jnp.exp2(s - top)
        total = jnp.sum(wt, axis=0, keepdims=True)
        turned = lax.dot_general(eye, vals, NT, preferred_element_type=jnp.float32).astype(jnp.bfloat16)
        part = jnp.dot(turned, wt.astype(jnp.bfloat16), preferred_element_type=jnp.float32)
        return part, top, total

    def units(o, half):
        num, top, total = fresh(o)
        return [
            merge(unit(o, d), (num, jnp.where(z == d, top, DEAD), total)) for d in range(4 * half, 4 * half + 4)
        ]

    row16 = iota((16, 128), 0)

    def back(direction, k, half):
        target = dev(z_dn if direction == 0 else z_up, c, y)
        return remote(
            rs_out.at[direction, k - 1, half], rs_in.at[direction, k - 1, half],
            rss.at[direction, k - 1, half], rsr.at[direction, k - 1, half], target,
        )

    def unpack(direction, k, half):
        st = rs_in[direction, k - 1, half, 512:528, :].astype(jnp.float32)
        return [
            (
                rs_in[direction, k - 1, half, 128 * i : 128 * i + 128, :].astype(jnp.float32),
                st[3 * i : 3 * i + 1],
                st[3 * i + 1 : 3 * i + 2] + st[3 * i + 2 : 3 * i + 3],
            )
            for i in range(4)
        ]

    def give(direction, k, half, o, merged):
        parts = units(o, half)
        if merged:
            back(direction, k + 1, half).wait_recv()
            parts = [merge(a, b) for a, b in zip(parts, unpack(direction, k + 1, half))]
        stats = jnp.zeros((16, 128), jnp.float32)
        for i, (num, top, total) in enumerate(parts):
            top_b = top.astype(jnp.bfloat16).astype(jnp.float32)
            shift = jnp.exp2(top - top_b)
            top, total = top_b, total * shift
            rs_out[direction, k - 1, half, 128 * i : 128 * i + 128, :] = (num * shift).astype(jnp.bfloat16)
            total_hi = total.astype(jnp.bfloat16).astype(jnp.float32)
            for n, values in enumerate((top, total_hi, total - total_hi)):
                stats = jnp.where(row16 == 3 * i + n, values, stats)
        rs_out[direction, k - 1, half, 512:528, :] = stats.astype(jnp.bfloat16)
        back(direction, k, half).start()

    for direction in range(2):
        give(direction, 4, direction, wrap(z + 4, 8), False)
    for k in (3, 2, 1):
        for n in range(2):
            for direction in range(2):
                half = 1 - direction if n == 0 else direction
                give(direction, k, half, wrap(z - k if direction == 0 else z + k, 8), k < 3 or n == 1)

    ds = 8 // NG

    def rows_of(ref, r):
        return ref.at[:, pl.ds(r * ds, ds)]

    def gather(direction, step, r):
        sign = 1 if direction == 0 else -1
        o = wrap(z - sign * (step - 1), 8)
        ref = g.at[c, o]
        ref = rows_of(ref, r) if step < 4 else ref.at[pl.ds(2 * direction, 2), pl.ds(r * ds, ds)]
        target = dev(z_up if direction == 0 else z_dn, c, y)
        return remote(ref, ref, zs.at[direction, step - 1, r], zr.at[direction, step - 1, r], target)

    def across(dz, r):
        ref = rows_of(g.at[c, wrap(z + dz, 8)], r)
        return remote(ref, ref, ks.at[dz, r], kr.at[dz, r], dev(z, 1 - c, y))

    def start_gather(r):
        for direction in range(2):
            gather(direction, 1, r).start()

    parts = units(z, 0) + units(z, 1)
    for half in range(2):
        for direction in range(2):
            back(direction, 1, half).wait_recv()
        below, above = unpack(0, 1, half), unpack(1, 1, half)
        for i in range(4):
            d = 4 * half + i
            num, _, total = merge(merge(parts[d], below[i]), above[i])
            rows = jnp.transpose(num / total).astype(jnp.bfloat16)
            for h in range(4):
                g[c, z, h, d] = rows[h * 32 : (h + 1) * 32]
            if (d + 1) % ds == 0:
                r = d // ds
                if r < 2:
                    start_gather(r)
                across(0, r).start()

    for k in range(1, 8):
        spread(k).wait_send()
        match_copy(k).wait_send()
        new_copy(k).wait_send()
    for n in range(4):
        for direction in range(2):
            q_y(direction, n).wait_send()
            q_far(direction, n).wait_send()
            y_copy(direction, n).wait_send()
        for dy in range(4):
            q_core(dy, n).wait_send()
            if dy != 2:
                core_copy(dy, n).wait_send()
    for n in range(6):
        y_far(n // 3, n % 3).wait_send()
        core_copy(2, n).wait_send()
    for direction in range(2):
        for step in range(1, 5):
            around(direction, step).wait_send()
        for k in (1, 2, 3):
            for half in range(2):
                back(direction, k, half).wait_send()
        back(direction, 4, direction).wait_send()

    w_copy.wait()

    def exchange(dx, r):
        return remote(
            xs.at[dx - 1, r], xr.at[dx - 1, r], xss.at[dx - 1, r], xsr.at[dx - 1, r], {"kv": wrap(kx + dx, 4)}
        )

    def use(o, r, first):
        o = wrap(o, 8)
        block = g[:, o, :, pl.ds(r * ds, ds)].reshape(2, 4, ds * 32, 128)
        left = jnp.concatenate(
            [jnp.concatenate([block[cc, h] for h in range(4)], axis=1) for cc in range(2)], axis=0
        )
        step = jnp.dot(
            left, w[pl.ds(pl.multiple_of(o * 512, 512), 512), :], preferred_element_type=jnp.float32
        )
        if first:
            acc[r] = step
        else:
            acc[r] += step

    def send_sums(r):
        for dx in range(1, 4):
            kk = wrap(kx + dx, 4)
            xs[dx - 1, r] = acc[r, :, pl.ds(pl.multiple_of(kk * 256, 256), 256)].astype(jnp.bfloat16)
            exchange(dx, r).start()

    def add_sums(r):
        total = acc[r, :, pl.ds(pl.multiple_of(kx * 256, 256), 256)]
        for dx in range(1, 4):
            exchange(dx, r).wait_recv()
            total = total + xr[dx - 1, r].astype(jnp.float32)
        out[:, pl.ds(r * ds, ds)] = total.astype(jnp.bfloat16).reshape(2, ds, 32, 256)

    for r in range(NG):
        across(0, r).wait_recv()
        use(z, r, True)
    waiting = []

    def settle(left):
        while len(waiting) > left:
            dz, r = waiting.pop(0)
            across(dz % 8, r).wait_recv()
            use(z + dz, r, False)
            if dz == 4:
                send_sums(r)
                if r > 0:
                    add_sums(r - 1)

    for slot in range(1, 4 + NG):
        if 2 <= slot + 1 < NG:
            start_gather(slot + 1)
        for r in reversed(range(NG)):
            step = slot - r
            if not 1 <= step <= 4:
                continue
            for direction in range(2):
                gather(direction, step, r).wait_recv()
                if step < 4:
                    gather(direction, step + 1, r).start()
            for dz in (-step, step) if step < 4 else (4,):
                across(dz % 8, r).start()
                waiting.append((dz, r))
            settle(4 if step < 4 else 1)
    settle(0)
    add_sums(NG - 1)

    for r in range(NG):
        for direction in range(2):
            for step in range(1, 5):
                gather(direction, step, r).wait_send()
        for dz in range(8):
            across(dz, r).wait_send()
        for dx in range(1, 4):
            exchange(dx, r).wait_send()


def decode(*args):
    bf, f32 = jnp.bfloat16, jnp.float32
    vm = pltpu.VMEM
    dma = pltpu.SemaphoreType.DMA
    rows_g = 512 // NG
    return pl.pallas_call(
        kernel,
        out_shape=jax.ShapeDtypeStruct((2, 8, 32, 256), bf),
        in_specs=[pl.BlockSpec(memory_space=pltpu.HBM)] * 8,
        out_specs=pl.BlockSpec(memory_space=pltpu.VMEM),
        scratch_shapes=[
            vm((8, 4, 32, 128), bf),
            vm((128, 128), bf),
            vm((8, 32), jnp.int32),
            vm((1, 8), jnp.int32),
            vm((1, 8), jnp.int32),
            vm((1, 64), jnp.int32),
            vm((1024, 128), f32),
            vm((8, 10, 16, 128), bf),
            vm((8, 8, 10, 16, 128), bf),
            vm((8, 8, 8, 16, 128), bf),
            vm((8, 16, 128), bf),
            vm((8, 16, 128), bf),
            vm((8, 1, 128), jnp.int32),
            pltpu.SMEM((8, 1, 128), jnp.int32),
            vm((2, 16, 2, 2, PAGE, 128), bf),
            vm((2, 16, 2, 2, PAGE, 128), bf),
            vm((2, 16, 2, 2, PAGE, 128), bf),
            vm((2, 16, 2, 2, PAGE, 128), bf),
            vm((8, 2, 512, 128), bf),
            vm((8, 2, 128, 512), bf),
            vm((8, 512, 128), f32),
            vm((2, 4, 2, 528, 128), bf),
            vm((2, 4, 2, 528, 128), bf),
            vm((4096, 1024), bf),
            vm((2, 8, 4, 8, 32, 128), bf),
            vm((NG, rows_g, 1024), f32),
            vm((3, NG, rows_g, 256), bf),
            vm((3, NG, rows_g, 256), bf),
            dma((9,)),
            dma((8,)), dma((8,)),
            dma((8,)), dma((8,)),
            dma((8,)), dma((8,)),
            dma((2, 4)), dma((2, 4)),
            dma((2, 4)), dma((2, 4)),
            dma((4, 4)), dma((4, 4)),
            dma((2, 4)), dma((2, 4)),
            dma((2, 3)), dma((2, 3)),
            dma((4, 6)), dma((4, 6)),
            dma((2, 4)), dma((2, 4)),
            dma((2, 4, 2)), dma((2, 4, 2)),
            dma((2, 4, NG)), dma((2, 4, NG)),
            dma((8, NG)), dma((8, NG)),
            dma((3, NG)), dma((3, NG)),
        ],
        compiler_params=pltpu.CompilerParams(
            collective_id=1, has_side_effects=True, vmem_limit_bytes=60 * MIB
        ),
        name="decode",
    )(*args)


def body(prefill_kv, page_match, queries, new_kv, slot_request, page_table, context_len, out_weight):
    out = decode(
        queries, new_kv.reshape(128, HD), page_table.reshape(8, MAXP), context_len.reshape(1, 8),
        slot_request.reshape(1, 8), page_match.reshape(1, 64), prefill_kv, out_weight,
    )
    out = out.reshape(2, 8, 4, 8, 256).transpose(1, 0, 3, 2, 4)
    return out.reshape(128, 1, STEPS, 256)


def solution(mesh):
    in_specs = (
        P(("pre", "grp"), None, "kv", None, None),
        P(("pre", "grp"), None, None),
        P(("pre", "grp"), None, "kv", None),
        P(("pre", "grp"), None, None, "kv", None),
        P("pre", "grp"),
        P("pre", "grp", None),
        P("pre", "grp"),
        P("kv", "pre"),
    )
    out_specs = P(None, "grp", None, ("pre", "kv"))
    return jax.shard_map(body, mesh=mesh, in_specs=in_specs, out_specs=out_specs, check_vma=False)
```

```python
import functools

import jax
import jax.numpy as jnp
from jax import lax
from jax.experimental import pallas as pl
from jax.experimental.pallas import tpu as pltpu
from jax.sharding import PartitionSpec as P

MESH = pl.DeviceIdType.MESH
HD = 128
PAGE = 64
STEPS = 4
MAXP = 32
NZ = 8
NM = 8
LOG2E = 1.4426950408889634
SCALE = LOG2E / HD**0.5
DEAD = -float(2**100)
MIB = 1 << 20
NG = 4
GROUPS = ((0, 2), (2, 2), (4, 2), (6, 2))
PAIRS = (0, 3, 1, 2)
CHUNKS = (((0, 2), (2, 4), (6, 2), (8, 8)), ((8, 2), (10, 4), (14, 2), (0, 8)))
NT = (((1,), (1,)), ((), ()))


def here():
    p = lax.axis_index("pre")
    return p // 2, p % 2, lax.axis_index("grp")


def dev(z, c, y):
    return {"pre": z * 2 + c, "grp": y}


def dev_zm(z, m):
    return dev(z, m // 4, m % 4)


def wrap(a, n):
    return lax.rem(a + 2 * n, n)


def remote(src, dst, ssem, rsem, device):
    return pltpu.make_async_remote_copy(
        src_ref=src, dst_ref=dst, send_sem=ssem, recv_sem=rsem, device_id=device, device_id_type=MESH
    )


def rank(rel):
    return 0 if rel == 0 else 1 if rel == 4 else 8 - 2 * rel if rel < 4 else 2 * rel - 7


def merge(a, b):
    acc_a, m_a, l_a = a
    acc_b, m_b, l_b = b
    top = jnp.maximum(m_a, m_b)
    fa = jnp.exp2(m_a - top)
    fb = jnp.exp2(m_b - top)
    return acc_a * fa + acc_b * fb, top, l_a * fa + l_b * fb


def ranks(rel):
    side = jnp.where(rel < 4, 8 - 2 * rel, 2 * rel - 7)
    return jnp.where(rel == 0, 0, jnp.where(rel == 4, 1, side))


def iota(shape, dim):
    return lax.broadcasted_iota(jnp.int32, shape, dim)


def one_hot(mask):
    return mask.astype(jnp.float32).astype(jnp.bfloat16)


def kernel(
    q_hbm, new_hbm, table_hbm, len_hbm, req_hbm, match_hbm, pg_hbm, w_hbm, out,
    q_in, new_in, table_in, len_in, req_in, match_in,
    qf, qx, i1, qg, ng, nh, mmv, mms, pages0, pages1, pages2, pages3, kd, vt, bi, rs_out, rs_in, w, g, acc, xs, xr,
    loc, sps, spr, nhs, nhr, mss, msr, qys, qyr, qfs, qfr, qcs, qcr, ys, yr, ys2, yr2, cs, cr, as_, ar, rss, rsr,
    zs, zr, ks, kr, xss, xsr,
):
    z, c, y = here()
    kx = lax.axis_index("kv")
    me_m = c * 4 + y
    z_up, z_dn = wrap(z + 1, 8), wrap(z - 1, 8)
    y_up, y_dn = wrap(y + 1, 4), wrap(y - 1, 4)

    loads = [
        pltpu.make_async_copy(src, dst, loc.at[3 + n])
        for n, (src, dst) in enumerate(
            (
                (q_hbm, q_in), (new_hbm, new_in), (table_hbm, table_in), (len_hbm, len_in), (req_hbm, req_in),
                (match_hbm, match_in),
            )
        )
    ]
    for load in loads:
        load.start()
    bar = pltpu.get_barrier_semaphore()
    for k in range(1, 8):
        pl.semaphore_signal(bar, inc=1, device_id=dev(wrap(z + k, 8), c, y), device_id_type=MESH)
        pl.semaphore_signal(bar, inc=1, device_id=dev_zm(z, wrap(me_m + k, 8)), device_id_type=MESH)
    for dx in range(1, 4):
        pl.semaphore_signal(bar, inc=1, device_id={"kv": wrap(kx + dx, 4)}, device_id_type=MESH)
    pages_at = (pages0, pages1, pages2, pages3)
    own_pages = pltpu.make_async_copy(pg_hbm, pages0.at[c], loc.at[0])
    own_pages.start()
    w_copy = pltpu.make_async_copy(w_hbm, w, loc.at[2])
    w_copy.start()

    for load in loads:
        load.wait()
    qf[0:1024, :] = q_in[...].reshape(1024, 128).astype(jnp.float32)

    def arrange(zj, carry):
        for tile in range(8):
            h, t = tile // 2, 2 * (tile % 2)
            rows = [qf[pl.ds((t + k) * 32 + 4 * zj + h, 8, stride=128), :] for k in range(2)]
            qx[zj, tile] = jnp.concatenate(rows, axis=0).astype(jnp.bfloat16)
        return carry

    lax.fori_loop(0, 8, arrange, 0)
    row = iota((128, 128), 0)
    lane = iota((128, 128), 1)
    origin = (row % 8) * 16 + ((row // 8) % 4) * 4 + ((row // 32) % 2) * 2 + row // 64
    new = jnp.dot(one_hot(origin == lane), new_in[...], preferred_element_type=jnp.float32).astype(jnp.bfloat16)
    lane8 = iota((8, 128), 1)
    facts = jnp.concatenate([table_in[...], jnp.zeros((8, 128 - MAXP), jnp.int32)], axis=1)

    def to_column(ref):
        line = jnp.concatenate([ref[...], jnp.zeros((1, 120), jnp.int32)], axis=1)
        line = jnp.where(lane8 == iota((8, 128), 0), jnp.broadcast_to(line, (8, 128)), 0)
        return jnp.broadcast_to(jnp.sum(line, axis=1, keepdims=True), (8, 128))

    length = to_column(len_in)
    request = to_column(req_in)
    for n, values in enumerate((length >> 6, length & 63, request >> 3, request & 7)):
        facts = jnp.where(lane8 == MAXP + n, values, facts)
    facts = facts.astype(jnp.float32)
    facts = jnp.concatenate([facts, facts], axis=0).astype(jnp.bfloat16)
    for zj in range(8):
        qx[zj, 8] = new[16 * zj : 16 * zj + 16]
        qx[zj, 9] = facts
    i1[me_m, 0] = qx[z]
    mmv[me_m] = jnp.concatenate([match_in[...], jnp.zeros((1, 64), jnp.int32)], axis=1)
    pl.semaphore_wait(bar, 17)

    def spread(kz):
        zj = wrap(z + kz, 8)
        return remote(qx.at[zj], i1.at[me_m, rank(8 - kz)], sps.at[kz], spr.at[rank(8 - kz)], dev(zj, c, y))

    def match_copy(km):
        return remote(mmv.at[me_m], mmv.at[me_m], mss.at[km], msr.at[km], dev_zm(z, wrap(me_m + km, 8)))

    def m_of(cc, yy):
        return cc * 4 + wrap(yy, 4)

    def y_dev(direction):
        return dev(z, c, y_up if direction == 0 else y_dn)

    def m_behind(direction):
        return m_of(c, y - 1 if direction == 0 else y + 1)

    def part(m, gi, tile, tiles):
        lo, n = GROUPS[gi]
        return i1.at[m, pl.ds(lo, n), pl.ds(tile, tiles)]

    def q_y(direction, gi):
        ref = part(me_m, gi, 0, 9)
        return remote(ref, ref, qys.at[direction, gi], qyr.at[direction, gi], y_dev(direction))

    def q_far(direction, gi):
        ref = part(m_behind(direction), gi, 5 * direction, 5 - direction)
        return remote(ref, ref, qfs.at[direction, gi], qfr.at[direction, gi], y_dev(direction))

    def q_core(dy, gi):
        ref = part(m_of(c, y + dy), gi, 0, 9)
        return remote(ref, ref, qcs.at[dy, gi], qcr.at[dy, gi], dev(z, 1 - c, y))

    behind = (3, 1)

    def chunk(dy, lo, n):
        return pages_at[dy].at[c, pl.ds(lo, n)]

    def y_copy(direction, n):
        lo, count = CHUNKS[direction][n]
        return remote(
            chunk(0, lo, count), chunk(behind[direction], lo, count),
            ys.at[direction, n], yr.at[direction, n], y_dev(direction),
        )

    def y_far(direction, n):
        lo, count = CHUNKS[direction][n]
        return remote(
            chunk(behind[direction], lo, count), chunk(2, lo, count),
            ys2.at[direction, n], yr2.at[direction, n], y_dev(direction),
        )

    def core_copy(dy, n):
        lo, count = ((CHUNKS[0][:3] + CHUNKS[1][:3]) if dy == 2 else CHUNKS[1 if dy == 1 else 0])[n]
        return remote(chunk(dy, lo, count), chunk(dy, lo, count), cs.at[dy, n], cr.at[dy, n], dev(z, 1 - c, y))

    for kz in (4, 3, 5, 2, 6, 1, 7):
        spread(kz).start()
    for km in range(1, 8):
        match_copy(km).start()

    def send_group(gi):
        q_y(0, gi).start()
        q_y(1, gi).start()
        q_core(0, gi).start()

    def send_pages(n):
        for direction in range(2):
            y_copy(direction, n).start()

    def forward_pages(n):
        for direction in range(2):
            y_copy(direction, n).wait_recv()
            if n < 3:
                y_far(direction, n).start()
            core_copy(behind[direction], n).start()

    own_pages.wait()
    send_pages(0)
    for gi in range(4):
        lo, n = GROUPS[gi]
        for rk in range(max(lo, 1), lo + n):
            kz = [k for k in range(1, 8) if rank(8 - k) == rk][0]
            spread(kz).wait_recv()
        send_group(gi)
    send_pages(1)
    for gi in range(4):
        for direction in range(2):
            q_y(direction, gi).wait_recv()
            q_far(direction, gi).start()
            q_core(behind[direction], gi).start()
    forward_pages(0)
    send_pages(2)
    send_pages(3)
    for n in range(4):
        core_copy(0, n).start()

    def biases(d, carry):
        rows = i1[me_m, from_plane(d), 9].astype(jnp.float32)
        rows = jnp.transpose(jnp.concatenate([rows] * 8, axis=0))
        pages = rows[0:32]
        whole = rows[32:33]
        rest = rows[33:34]
        slot = iota((32, 128), 0).astype(jnp.float32)
        before = (slot < whole).astype(jnp.float32)
        at = (slot == whole).astype(jnp.float32)
        within = iota((PAGE, 128), 0).astype(jnp.float32) < rest
        for m in range(8):
            number = z * 8 + m_of(m % 2, y + PAIRS[m // 2])
            same = (pages == number.astype(jnp.float32)).astype(jnp.float32)
            full = jnp.sum(same * before, axis=0, keepdims=True)
            more = full + jnp.sum(same * at, axis=0, keepdims=True)
            low = jnp.where(full > 0.0, jnp.log(jnp.maximum(full, 1.0)) * LOG2E, DEAD)
            high = jnp.where(more > 0.0, jnp.log(jnp.maximum(more, 1.0)) * LOG2E, DEAD)
            bi[d, m * PAGE : (m + 1) * PAGE, :] = jnp.where(within, high, low)
        return carry

    def from_plane(d):
        rel = wrap(d - z, 8)
        return ranks(rel)

    for gi in range(4):
        for direction in range(2):
            q_far(direction, gi).wait_recv()
        q_core(2, gi).start()
    for gi in range(4):
        for dy in (0, 1, 3, 2):
            q_core(dy, gi).wait_recv()

    facts = jnp.concatenate([i1[me_m, from_plane(d), 9] for d in range(8)], axis=0).astype(jnp.float32)
    source = facts[:, 34:35].astype(jnp.int32)
    within = facts[:, 35:36].astype(jnp.int32)
    rel = ((source >> 3) - z + 8) & 7
    ranked = ranks(rel)
    column = ((source & 7) * 8 + ranked) * 16 + within
    column = jnp.broadcast_to(column, (128, 1024)) + (iota((128, 1024), 0) & 8)
    hot = one_hot(column == iota((128, 1024), 1))
    for fp in range(9):
        rows = jnp.dot(
            hot, i1[:, :, fp].reshape(1024, 128), preferred_element_type=jnp.float32
        ).astype(jnp.bfloat16).reshape(8, 16, 128)
        if fp < 8:
            qg[z, fp] = rows
        else:
            ng[...] = rows

    def around(direction, step):
        sign = 1 if direction == 0 else -1
        o = wrap(z - sign * (step - 1), 8)
        ref = qg.at[o] if step < 4 else qg.at[o, :, pl.ds(4 * direction, 4)]
        target = dev(z_up if direction == 0 else z_dn, c, y)
        return remote(ref, ref, as_.at[direction, step - 1], ar.at[direction, step - 1], target)

    def pass_on(step):
        for direction in range(2):
            around(direction, step).wait_recv()
            around(direction, step + 1).start()

    for direction in range(2):
        around(direction, 1).start()

    def new_copy(kz):
        zj = wrap(z + kz, 8)
        return remote(ng.at[zj], nh.at[z], nhs.at[kz], nhr.at[kz], dev(zj, c, y))

    for kz in range(1, 8):
        new_copy(kz).start()
    nh[z] = ng[z]

    lax.fori_loop(0, 8, biases, 0)
    eye = one_hot(row == lane)

    def select_pages(pair):
        dy = PAIRS[pair]

        def one(d, carry):
            picks = [mms[m_of(k, y + dy), 0, d * 8 + me_m] for k in range(2)]
            for h in range(2):
                values = []
                for k in range(2):
                    m = 2 * pair + k
                    kd[d, h, m * PAGE : (m + 1) * PAGE, :] = pages_at[dy][k, picks[k], 0, h]
                    values.append(pages_at[dy][k, picks[k], 1, h])
                turned = lax.dot_general(
                    eye, jnp.concatenate(values, axis=0), NT, preferred_element_type=jnp.float32
                )
                vt[d, h, :, pair * 128 : (pair + 1) * 128] = turned.astype(jnp.bfloat16)
            return carry

        lax.fori_loop(0, 8, one, 0)

    def wait_cores(dy):
        for n in range(6 if dy == 2 else 4):
            core_copy(dy, n).wait_recv()

    for km in range(1, 8):
        match_copy(km).wait_recv()
    to_smem = pltpu.make_async_copy(mmv, mms, loc.at[1])
    to_smem.start()
    forward_pages(1)
    to_smem.wait()
    wait_cores(0)
    select_pages(0)
    pass_on(1)
    forward_pages(2)
    pass_on(2)
    forward_pages(3)
    wait_cores(3)
    select_pages(1)
    wait_cores(1)
    select_pages(2)
    pass_on(3)
    for n in range(3):
        for direction in range(2):
            y_far(direction, n).wait_recv()
            core_copy(2, 3 * direction + n).start()
    wait_cores(2)
    select_pages(3)
    for direction in range(2):
        around(direction, 4).wait_recv()
    for kz in range(1, 8):
        new_copy(kz).wait_recv()

    def unit(o, d):
        h = o // 4
        q = qg[o, :, d].reshape(128, 128)
        s = lax.dot_general(kd[d, h], q, NT, preferred_element_type=jnp.float32)
        s = s * SCALE + bi[d]
        top = jnp.max(s, axis=0, keepdims=True)
        wt = jnp.exp2(s - top)
        total = jnp.sum(wt, axis=0, keepdims=True)
        part = jnp.dot(vt[d, h], wt.astype(jnp.bfloat16), preferred_element_type=jnp.float32)
        return part, top, total

    nrow = iota((32, 128), 0)
    nlane = iota((32, 128), 1)
    valid = (nrow % 8 == nlane % 8) & (nrow // 8 <= (nlane // 8) % 4)

    def fresh(o):
        h = o // 4
        q = qg[o, :, z].reshape(128, 128)
        keys = nh[pl.ds(4 * h, 2)].reshape(32, 128)
        vals = nh[pl.ds(4 * h + 2, 2)].reshape(32, 128)
        s = lax.dot_general(keys, q, NT, preferred_element_type=jnp.float32) * SCALE
        s = jnp.where(valid, s, DEAD)
        top = jnp.max(s, axis=0, keepdims=True)
        wt = jnp.exp2(s - top)
        total = jnp.sum(wt, axis=0, keepdims=True)
        turned = lax.dot_general(eye, vals, NT, preferred_element_type=jnp.float32).astype(jnp.bfloat16)
        part = jnp.dot(turned, wt.astype(jnp.bfloat16), preferred_element_type=jnp.float32)
        return part, top, total

    def units(o, half):
        num, top, total = fresh(o)
        return [
            merge(unit(o, d), (num, jnp.where(z == d, top, DEAD), total)) for d in range(4 * half, 4 * half + 4)
        ]

    row16 = iota((16, 128), 0)

    def back(direction, k, half):
        target = dev(z_dn if direction == 0 else z_up, c, y)
        return remote(
            rs_out.at[direction, k - 1, half], rs_in.at[direction, k - 1, half],
            rss.at[direction, k - 1, half], rsr.at[direction, k - 1, half], target,
        )

    def unpack(direction, k, half):
        st = rs_in[direction, k - 1, half, 512:528, :].astype(jnp.float32)
        return [
            (
                rs_in[direction, k - 1, half, 128 * i : 128 * i + 128, :].astype(jnp.float32),
                st[3 * i : 3 * i + 1],
                st[3 * i + 1 : 3 * i + 2] + st[3 * i + 2 : 3 * i + 3],
            )
            for i in range(4)
        ]

    def give(direction, k, half, o, merged):
        parts = units(o, half)
        if merged:
            back(direction, k + 1, half).wait_recv()
            parts = [merge(a, b) for a, b in zip(parts, unpack(direction, k + 1, half))]
        stats = jnp.zeros((16, 128), jnp.float32)
        for i, (num, top, total) in enumerate(parts):
            top_b = top.astype(jnp.bfloat16).astype(jnp.float32)
            shift = jnp.exp2(top - top_b)
            top, total = top_b, total * shift
            rs_out[direction, k - 1, half, 128 * i : 128 * i + 128, :] = (num * shift).astype(jnp.bfloat16)
            total_hi = total.astype(jnp.bfloat16).astype(jnp.float32)
            for n, values in enumerate((top, total_hi, total - total_hi)):
                stats = jnp.where(row16 == 3 * i + n, values, stats)
        rs_out[direction, k - 1, half, 512:528, :] = stats.astype(jnp.bfloat16)
        back(direction, k, half).start()

    for direction in range(2):
        give(direction, 4, direction, wrap(z + 4, 8), False)
    for k in (3, 2, 1):
        for n in range(2):
            for direction in range(2):
                half = 1 - direction if n == 0 else direction
                give(direction, k, half, wrap(z - k if direction == 0 else z + k, 8), k < 3 or n == 1)

    ds = 8 // NG

    def rows_of(ref, r):
        return ref.at[:, pl.ds(r * ds, ds)]

    def gather(direction, step, r):
        sign = 1 if direction == 0 else -1
        o = wrap(z - sign * (step - 1), 8)
        ref = g.at[c, o]
        ref = rows_of(ref, r) if step < 4 else ref.at[pl.ds(2 * direction, 2), pl.ds(r * ds, ds)]
        target = dev(z_up if direction == 0 else z_dn, c, y)
        return remote(ref, ref, zs.at[direction, step - 1, r], zr.at[direction, step - 1, r], target)

    def across(dz, r):
        ref = rows_of(g.at[c, wrap(z + dz, 8)], r)
        return remote(ref, ref, ks.at[dz, r], kr.at[dz, r], dev(z, 1 - c, y))

    def start_gather(r):
        for direction in range(2):
            gather(direction, 1, r).start()

    parts = units(z, 0) + units(z, 1)
    for k in range(1, 8):
        spread(k).wait_send()
        match_copy(k).wait_send()
        new_copy(k).wait_send()
    for n in range(4):
        for direction in range(2):
            q_y(direction, n).wait_send()
            q_far(direction, n).wait_send()
            y_copy(direction, n).wait_send()
        for dy in range(4):
            q_core(dy, n).wait_send()
            if dy != 2:
                core_copy(dy, n).wait_send()
    for n in range(6):
        y_far(n // 3, n % 3).wait_send()
        core_copy(2, n).wait_send()
    for direction in range(2):
        for step in range(1, 5):
            around(direction, step).wait_send()

    for half in range(2):
        for direction in range(2):
            back(direction, 1, half).wait_recv()
        below, above = unpack(0, 1, half), unpack(1, 1, half)
        for i in range(4):
            d = 4 * half + i
            num, _, total = merge(merge(parts[d], below[i]), above[i])
            rows = jnp.transpose(num / total).astype(jnp.bfloat16)
            for h in range(4):
                g[c, z, h, d] = rows[h * 32 : (h + 1) * 32]
            if (d + 1) % ds == 0:
                r = d // ds
                if r < 2:
                    start_gather(r)
                across(0, r).start()

    w_copy.wait()

    def exchange(dx, r):
        return remote(
            xs.at[dx - 1, r], xr.at[dx - 1, r], xss.at[dx - 1, r], xsr.at[dx - 1, r], {"kv": wrap(kx + dx, 4)}
        )

    def use(o, r, first):
        o = wrap(o, 8)
        block = g[:, o, :, pl.ds(r * ds, ds)].reshape(2, 4, ds * 32, 128)
        left = jnp.concatenate(
            [jnp.concatenate([block[cc, h] for h in range(4)], axis=1) for cc in range(2)], axis=0
        )
        step = jnp.dot(
            left, w[pl.ds(pl.multiple_of(o * 512, 512), 512), :], preferred_element_type=jnp.float32
        )
        if first:
            acc[r] = step
        else:
            acc[r] += step

    def send_sums(r):
        for dx in range(1, 4):
            kk = wrap(kx + dx, 4)
            xs[dx - 1, r] = acc[r, :, pl.ds(pl.multiple_of(kk * 256, 256), 256)].astype(jnp.bfloat16)
            exchange(dx, r).start()

    def add_sums(r):
        total = acc[r, :, pl.ds(pl.multiple_of(kx * 256, 256), 256)]
        for dx in range(1, 4):
            exchange(dx, r).wait_recv()
            total = total + xr[dx - 1, r].astype(jnp.float32)
        out[:, pl.ds(r * ds, ds)] = total.astype(jnp.bfloat16).reshape(2, ds, 32, 256)

    waiting = [(0, r) for r in range(NG)]

    def settle(left):
        while len(waiting) > left:
            dz, r = waiting.pop(0)
            across(dz % 8, r).wait_recv()
            use(z + dz, r, dz == 0)
            if dz == 4:
                send_sums(r)
                if r > 0:
                    add_sums(r - 1)

    for slot in range(1, 4 + NG):
        if 2 <= slot + 1 < NG:
            start_gather(slot + 1)
        for r in reversed(range(NG)):
            step = slot - r
            if not 1 <= step <= 4:
                continue
            for direction in range(2):
                gather(direction, step, r).wait_recv()
                if step < 4:
                    gather(direction, step + 1, r).start()
            for dz in (-step, step) if step < 4 else (4,):
                across(dz % 8, r).start()
                waiting.append((dz, r))
            settle(4 if step < 4 else 1)
    settle(0)
    for direction in range(2):
        for k in (1, 2, 3):
            for half in range(2):
                back(direction, k, half).wait_send()
        back(direction, 4, direction).wait_send()
    for r in range(NG):
        for direction in range(2):
            for step in range(1, 5):
                gather(direction, step, r).wait_send()
        for dz in range(8):
            across(dz, r).wait_send()
    add_sums(NG - 1)
    for r in range(NG):
        for dx in range(1, 4):
            exchange(dx, r).wait_send()


def decode(*args):
    bf, f32 = jnp.bfloat16, jnp.float32
    vm = pltpu.VMEM
    dma = pltpu.SemaphoreType.DMA
    rows_g = 512 // NG
    return pl.pallas_call(
        kernel,
        out_shape=jax.ShapeDtypeStruct((2, 8, 32, 256), bf),
        in_specs=[pl.BlockSpec(memory_space=pltpu.HBM)] * 8,
        out_specs=pl.BlockSpec(memory_space=pltpu.VMEM),
        scratch_shapes=[
            vm((8, 4, 32, 128), bf),
            vm((128, 128), bf),
            vm((8, 32), jnp.int32),
            vm((1, 8), jnp.int32),
            vm((1, 8), jnp.int32),
            vm((1, 64), jnp.int32),
            vm((1152, 128), f32),
            vm((8, 10, 16, 128), bf),
            vm((8, 8, 10, 16, 128), bf),
            vm((8, 8, 8, 16, 128), bf),
            vm((8, 16, 128), bf),
            vm((8, 16, 128), bf),
            vm((8, 1, 128), jnp.int32),
            pltpu.SMEM((8, 1, 128), jnp.int32),
            vm((2, 16, 2, 2, PAGE, 128), bf),
            vm((2, 16, 2, 2, PAGE, 128), bf),
            vm((2, 16, 2, 2, PAGE, 128), bf),
            vm((2, 16, 2, 2, PAGE, 128), bf),
            vm((8, 2, 512, 128), bf),
            vm((8, 2, 128, 512), bf),
            vm((8, 512, 128), f32),
            vm((2, 4, 2, 528, 128), bf),
            vm((2, 4, 2, 528, 128), bf),
            vm((4096, 1024), bf),
            vm((2, 8, 4, 8, 32, 128), bf),
            vm((NG, rows_g, 1024), f32),
            vm((3, NG, rows_g, 256), bf),
            vm((3, NG, rows_g, 256), bf),
            dma((9,)),
            dma((8,)), dma((8,)),
            dma((8,)), dma((8,)),
            dma((8,)), dma((8,)),
            dma((2, 4)), dma((2, 4)),
            dma((2, 4)), dma((2, 4)),
            dma((4, 4)), dma((4, 4)),
            dma((2, 4)), dma((2, 4)),
            dma((2, 3)), dma((2, 3)),
            dma((4, 6)), dma((4, 6)),
            dma((2, 4)), dma((2, 4)),
            dma((2, 4, 2)), dma((2, 4, 2)),
            dma((2, 4, NG)), dma((2, 4, NG)),
            dma((8, NG)), dma((8, NG)),
            dma((3, NG)), dma((3, NG)),
        ],
        compiler_params=pltpu.CompilerParams(
            collective_id=1, has_side_effects=True, vmem_limit_bytes=60 * MIB
        ),
        name="decode",
    )(*args)


def body(prefill_kv, page_match, queries, new_kv, slot_request, page_table, context_len, out_weight):
    out = decode(
        queries, new_kv.reshape(128, HD), page_table.reshape(8, MAXP), context_len.reshape(1, 8),
        slot_request.reshape(1, 8), page_match.reshape(1, 64), prefill_kv, out_weight,
    )
    out = out.reshape(2, 8, 4, 8, 256).transpose(1, 0, 3, 2, 4)
    return out.reshape(128, 1, STEPS, 256)


def solution(mesh):
    in_specs = (
        P(("pre", "grp"), None, "kv", None, None),
        P(("pre", "grp"), None, None),
        P(("pre", "grp"), None, "kv", None),
        P(("pre", "grp"), None, None, "kv", None),
        P("pre", "grp"),
        P("pre", "grp", None),
        P("pre", "grp"),
        P("kv", "pre"),
    )
    out_specs = P(None, "grp", None, ("pre", "kv"))
    return jax.shard_map(body, mesh=mesh, in_specs=in_specs, out_specs=out_specs, check_vma=False)
```
